32 devices in a mesh: gx: 8 (over z, core), gy: 4 (over y, x).
Axes of the slice: x: 2, y: 2, z: 4, core: 2. Of those that a mesh axis runs over, the one named last changes fastest.
Arguments:
- tokens: bfloat16 [2, 512, 197, 384], P(None, ('gx', 'gy')), may hold values from -6 to 6
- counts: int32 [32, 2], P(('gx', 'gy')), may hold values from 1 to 16, as said below
- cotangent: bfloat16 [2, 512, 197, 384], P(None, ('gx', 'gy')), may hold values from -6 to 6
- w_qkv: bfloat16 [442368], P(('gx', 'gy')), may hold values from -0.3125 to 0.3125
- w_out: bfloat16 [147456], P(('gx', 'gy')), may hold values from -0.625 to 0.625
- w_fc1: bfloat16 [589824], P(('gx', 'gy')), may hold values from -0.3125 to 0.3125
- w_fc2: bfloat16 [589824], P(('gx', 'gy')), may hold values from -0.15625 to 0.15625
- gains: bfloat16 [768], P(('gx', 'gy')), may hold values from 0.25 to 1.75
- shifts: bfloat16 [768], P(('gx', 'gy')), may hold values from -3 to 3
- biases: bfloat16 [3072], P(('gx', 'gy')), may hold values from -3 to 3
Outputs:
- result: bfloat16 [2, 512, 197, 384], P(None, ('gx', 'gy'))
- grad_tokens: bfloat16 [2, 512, 197, 384], P(None, ('gx', 'gy'))
- grad_qkv: float32 [442368], P(('gx', 'gy'))
- grad_out: float32 [147456], P(('gx', 'gy'))
- grad_fc1: float32 [589824], P(('gx', 'gy'))
- grad_fc2: float32 [589824], P(('gx', 'gy'))
- grad_gains: float32 [768], P(('gx', 'gy'))
- grad_shifts: float32 [768], P(('gx', 'gy'))
- grad_biases: float32 [3072], P(('gx', 'gy'))
The draws below stay inside these ranges and needn't reach their ends.
Inputs may be any that keep to these rules, and one draw needn't show every extreme that they name: `counts`: every device has at least one live image in each micro-batch, and some device has all 16 slots live.
All inputs are finite; a program needn't handle non-finite values.
Results may differ from the reference program's by a relative error of at most 0.0086.
Values may be sent and summed in bfloat16 or wider, within the bound.
No kernel may reach another device: no remote copies, remote signals or barrier semaphores. Data moves between devices by JAX's collectives and lax.ppermute only.
A program may use at most 384 MiB of HBM per device.

```python
import jax
import jax.numpy as jnp
from jax import lax

D = 384
HEADS = 6
HEAD = 64
FF = 1536
SEQ = 197
MB = 2
CAP = 16
IMAGES = 512
N_GX = 8
N_GY = 4


def draw_counts(key, part):
    key = jax.random.fold_in(key, 7)
    first_key, spot_key = jax.random.split(key)
    entries = N_GX * N_GY * MB
    drawn = jax.random.randint(first_key, (entries,), 1, CAP + 1, dtype=jnp.int32)
    spot = jax.random.randint(spot_key, (), 0, entries, dtype=jnp.int32)
    drawn = jnp.where(jnp.arange(entries, dtype=jnp.int32) == spot, CAP, drawn)
    return drawn.reshape(N_GX * N_GY, MB).astype(jnp.int32)


def block_levels(key, shape, cuts, smallest, high):
    level = 1.0
    for axis_at, shards_of in cuts:
        steps = jax.random.uniform(jax.random.fold_in(jax.random.fold_in(key, 6), axis_at), (shards_of,), jnp.float32, smallest / len(cuts), high / len(cuts))
        level = level * jnp.repeat(jnp.exp(steps), shape[axis_at] // shards_of).reshape((-1,) + (1,) * (len(shape) - 1 - axis_at))
    return level


def bell_draw(key, dims, scale, most, pieces=(), kind=jnp.bfloat16):
    values = jax.random.normal(key, dims, jnp.float32) * scale
    if len(pieces) > 0:
        values = block_levels(key, dims, pieces, -0.22, 0.18) * values
    return jnp.clip(values, min=-most, max=most).astype(kind)


def setup_inputs(seed: int = 0) -> dict:
    key_of = jax.random.split(jax.random.key(seed), 11)
    return {
        "tokens": bell_draw(key_of[0], (MB, IMAGES, SEQ, D), 1.0, 6.0, ((1, 32),)),
        "counts": draw_counts(jax.random.fold_in(key_of[10], 71), 0),
        "cotangent": bell_draw(key_of[2], (MB, IMAGES, SEQ, D), 1.0, 6.0, ((1, 32),)),
        "w_qkv": bell_draw(key_of[3], (3 * D * D,), D ** -0.5, 0.3125, ((0, 32),)),
        "w_out": bell_draw(key_of[4], (D * D,), (D // 4) ** -0.5, 0.625, ((0, 32),)),
        "w_fc1": bell_draw(key_of[5], (D * FF,), D ** -0.5, 0.3125, ((0, 32),)),
        "w_fc2": bell_draw(key_of[6], (FF * D,), FF ** -0.5, 0.15625, ((0, 32),)),
        "gains": jnp.clip(1.0 + 0.15 * jax.random.normal(key_of[7], (2 * D,), jnp.float32), 0.25, 1.75).astype(jnp.bfloat16),
        "shifts": bell_draw(key_of[8], (2 * D,), 0.5, 3.0, ((0, 32),)),
        "biases": bell_draw(key_of[9], (4 * D + FF,), 0.5, 3.0, ((0, 32),)),
    }


EPS = 1e-06
HIGH = lax.Precision.HIGHEST

@jax.custom_vjp
def low(v):
    return lax.optimization_barrier(v.astype(jnp.bfloat16)).astype(jnp.float32)

@jax.custom_vjp
def low_back(v):
    return v

def low_keep(v):
    return (low(v), None)

def low_pass(kept, grad):
    return (grad,)

def back_keep(v):
    return (v, None)

def back_low(kept, grad):
    return (low(grad),)
low.defvjp(low_keep, low_pass)
low_back.defvjp(back_keep, back_low)

def normalize(values, gain, shift):
    center = values - lax.optimization_barrier(jnp.mean(values, axis=-1, keepdims=True))
    spread = lax.optimization_barrier(jnp.mean(center * center, axis=-1, keepdims=True))
    return center * lax.rsqrt(spread + EPS) * gain + shift

def product(left, right):
    return jnp.matmul(left, right, precision=HIGH)

def block(inputs, live, w_qkv, w_out, w_fc1, w_fc2, gains, shifts, biases):
    images, length, width = inputs.shape
    hidden_units = w_fc1.shape[1]
    bias_query = biases[:width]
    bias_value = biases[width:2 * width]
    bias_out = biases[2 * width:3 * width]
    bias_hidden = biases[3 * width:3 * width + hidden_units]
    bias_last = biases[3 * width + hidden_units:]
    scale = HEAD ** (-0.5)
    normed = low(normalize(inputs, gains[:width], shifts[:width]))
    joined = product(normed, w_qkv)
    queries = low(low_back(joined[..., :width] + bias_query)).reshape(images, length, HEADS, HEAD)
    keys_all = low(low_back(joined[..., width:2 * width])).reshape(images, length, HEADS, HEAD)
    values_all = low(low_back(joined[..., 2 * width:] + bias_value)).reshape(images, length, HEADS, HEAD)
    scores = low_back(jnp.einsum('bqhd,bkhd->bhqk', queries, keys_all, precision=HIGH) * scale)
    attend = low(jax.nn.softmax(scores, axis=-1))
    mixed = jnp.einsum('bhqk,bkhd->bqhd', attend, values_all, precision=HIGH).reshape(images, length, width)
    mixed = low(low_back(mixed))
    branch = low_back(product(mixed, w_out) + bias_out)
    middle = inputs + branch
    normed_two = low(normalize(middle, gains[width:], shifts[width:]))
    hidden = low_back(product(normed_two, w_fc1) + bias_hidden)
    active = low(jax.nn.gelu(hidden, approximate=False))
    last = low_back(product(active, w_fc2) + bias_last)
    return (middle + last) * live[:, None, None]

def reference(tokens, counts, cotangent, w_qkv, w_out, w_fc1, w_fc2, gains, shifts, biases):
    devices = counts.shape[0]
    slots = (jnp.arange(CAP, dtype=jnp.int32)[None, None, :] < counts.T[:, :, None]).astype(jnp.float32)

    def forward(inputs, flat_qkv, flat_out, flat_fc1, flat_fc2, gain_all, shift_all, bias_all):
        matrix_qkv = flat_qkv.reshape(D, 3 * D)
        matrix_out = flat_out.reshape(D, D)
        matrix_fc1 = flat_fc1.reshape(D, FF)
        matrix_fc2 = flat_fc2.reshape(FF, D)
        groups = inputs.reshape(MB * devices, CAP, SEQ, D)
        lives = slots.reshape(MB * devices, CAP)

        def group_step(carry, item):
            output = jax.checkpoint(block)(item[0], item[1], matrix_qkv, matrix_out, matrix_fc1, matrix_fc2, gain_all, shift_all, bias_all)
            return (carry, output)
        _, outcome = lax.scan(group_step, None, (groups, lives))
        return outcome.reshape(MB, devices * CAP, SEQ, D)
    floats = [array.astype(jnp.float32) for array in (tokens, w_qkv, w_out, w_fc1, w_fc2, gains, shifts, biases)]
    outcome, pullback = jax.vjp(forward, *floats)
    grads = pullback(cotangent.astype(jnp.float32))
    return (outcome.astype(jnp.bfloat16), grads[0].astype(jnp.bfloat16), grads[1], grads[2], grads[3], grads[4], grads[5], grads[6], grads[7])
```

```python
import functools

import jax
import jax.numpy as jnp
from jax import lax
from jax.experimental import pallas as pl
from jax.experimental.pallas import tpu as pltpu
from jax.sharding import PartitionSpec as P

HEAD = 64
EPS = 1e-06
F32 = jnp.float32
B16 = jnp.bfloat16
AXES = ("gx", "gy")
GROUP = 2
LANES = 128


def round_up(value, unit):
    return -(-value // unit) * unit


def dot(left, right):
    return jnp.dot(left, right, preferred_element_type=F32)


def dot_t(left, right):
    return lax.dot_general(left, right, (((1,), (1,)), ((), ())), preferred_element_type=F32)


def t_dot(left, right):
    return lax.dot_general(left, right, (((0,), (0,)), ((), ())), preferred_element_type=F32)


def norm_parts(values):
    center = values - jnp.mean(values, axis=-1, keepdims=True)
    factor = lax.rsqrt(jnp.mean(center * center, axis=-1, keepdims=True) + EPS)
    return center * factor, factor


def norm_back(incoming, unit, factor, gain):
    scaled = incoming * gain
    return factor * (
        scaled
        - jnp.mean(scaled, axis=-1, keepdims=True)
        - unit * jnp.mean(scaled * unit, axis=-1, keepdims=True)
    )


def colsum(values):
    return jnp.sum(values, axis=0, keepdims=True)


def gelu_both(hidden):
    size = jnp.abs(hidden)
    t = 1.0 / (1.0 + (0.3275911 * 0.5**0.5) * size)
    bell = jnp.exp(-0.5 * hidden * hidden)
    poly = t * (
        0.127414796
        + t * (-0.142248368 + t * (0.7107068705 + t * (-0.7265760135 + t * 0.5307027145)))
    )
    tail = poly * bell
    area = jnp.where(hidden >= 0, 1.0 - tail, tail)
    return hidden * area, area + hidden * (bell * 0.3989422804014327)


def block_kernel(
    length,
    chunk,
    counts,
    tok,
    cot,
    w_qkv,
    w_out,
    w_fc1,
    w_fc2,
    vec,
    res,
    gtok,
    g_qkv,
    g_out,
    g_fc1,
    g_fc2,
    g_vec,
    x_s,
    dy_s,
    normed_s,
    qkv_s,
    attend_s,
    mixed_s,
    dmix_s,
    dj_s,
):
    width = tok.shape[-1]
    hidden_units = w_fc1.shape[1]
    rows = x_s.shape[0] // GROUP
    deep = qkv_s.shape[0] // GROUP
    pairs = width // LANES
    micro, place = pl.program_id(0), pl.program_id(1)
    live_count = counts[micro]

    @pl.when((micro == 0) & (place == 0))
    def _():
        for ref in (x_s, dy_s, qkv_s, dmix_s, g_qkv, g_out, g_fc1, g_fc2, g_vec):
            ref[...] = jnp.zeros_like(ref)

    @pl.when(place * GROUP >= live_count)
    def _():
        res[...] = jnp.zeros_like(res)
        gtok[...] = jnp.zeros_like(gtok)

    @pl.when(place * GROUP < live_count)
    def _():
        for i in range(GROUP):
            live = (place * GROUP + i < live_count).astype(F32)
            x_s[i * rows : i * rows + length] = tok[0, i].astype(F32)
            dy_s[i * rows : i * rows + length] = cot[0, i].astype(F32) * live
        gain_one, gain_two = vec[0:1, :width], vec[1:2, :width]
        shift_one, shift_two = vec[2:3, :width], vec[3:4, :width]
        bias_query, bias_value = vec[4:5, :width], vec[5:6, :width]
        bias_out, bias_last = vec[6:7, :width], vec[7:8, :width]

        unit_one, factor_one = norm_parts(x_s[...])
        normed_s[...] = (unit_one * gain_one + shift_one).astype(B16)
        scale = HEAD**-0.5
        queries = ((dot(normed_s[...], w_qkv[:, :width]) + bias_query) * scale).astype(B16)
        keys_all = dot(normed_s[...], w_qkv[:, width : 2 * width]).astype(B16)
        values_all = (dot(normed_s[...], w_qkv[:, 2 * width :]) + bias_value).astype(B16)
        for i in range(GROUP):
            for at, part in enumerate((queries, keys_all, values_all)):
                qkv_s[i * deep : i * deep + rows, at * width : (at + 1) * width] = part[
                    i * rows : (i + 1) * rows
                ]

        first_half = lax.broadcasted_iota(jnp.int32, (1, LANES), 1) < HEAD
        tail = rows - 16
        hide = jnp.where(
            lax.broadcasted_iota(jnp.int32, (16, 1), 0) + tail < length, 0.0, -1e30
        ).astype(F32)
        blank = jnp.zeros((deep - rows, deep), B16)

        def halves(two):
            zero = jnp.zeros_like(two)
            return jnp.where(first_half, two, zero), jnp.where(first_half, zero, two)

        for i in range(GROUP):
            for pair in range(pairs):
                lanes = pl.ds(pair * LANES, LANES)
                q2 = qkv_s[pl.ds(i * deep, deep), lanes]
                k2 = qkv_s[pl.ds(i * deep, rows), pl.ds(width + pair * LANES, LANES)]
                v2 = qkv_s[pl.ds(i * deep, deep), pl.ds(2 * width + pair * LANES, LANES)]
                v_t = v2.T
                parts = []
                for half, q_one in enumerate(halves(q2)):
                    scores = dot_t(k2, q_one)
                    scores = jnp.concatenate([scores[:tail], scores[tail:] + hide], axis=0)
                    scores = jnp.exp(scores - jnp.max(scores, axis=0, keepdims=True))
                    total = jnp.sum(scores, axis=0, keepdims=True)
                    attend = (scores * (1.0 / total)).astype(B16)
                    attend_s[i * 2 * pairs + 2 * pair + half] = attend
                    parts.append(
                        dot(
                            v_t[half * HEAD : (half + 1) * HEAD],
                            jnp.concatenate([attend, blank], axis=0),
                        )
                    )
                mixed_two = jnp.concatenate(parts, axis=0).T
                mixed_s[pl.ds(i * rows, rows), lanes] = mixed_two[:rows].astype(B16)

        middle = x_s[...] + dot(mixed_s[...], w_out[...]) + bias_out
        unit_two, factor_two = norm_parts(middle)
        normed_two = (unit_two * gain_two + shift_two).astype(B16)
        d_last = dy_s[...].astype(B16)
        last = bias_last
        d_normed_two = 0.0
        for at in range(0, hidden_units, chunk):
            cols = slice(at, at + chunk)
            hidden = dot(normed_two, w_fc1[:, cols]) + vec[8:9, cols]
            active, slope = gelu_both(hidden)
            active = active.astype(B16)
            last = last + dot(active, w_fc2[cols, :])
            d_hidden = dot_t(d_last, w_fc2[cols, :]) * slope
            g_vec[8:9, cols] += colsum(d_hidden)
            d_hidden = d_hidden.astype(B16)
            d_normed_two = d_normed_two + dot_t(d_hidden, w_fc1[:, cols])
            g_fc2[cols, :] += t_dot(active, d_last)
            g_fc1[:, cols] += t_dot(normed_two, d_hidden)
        result = middle + last
        for i in range(GROUP):
            live = (place * GROUP + i < live_count).astype(F32)
            res[0, i] = (result[i * rows : i * rows + length] * live).astype(B16)
        d_middle = dy_s[...] + norm_back(d_normed_two, unit_two, factor_two, gain_two)
        g_vec[1:2, :width] += colsum(d_normed_two * unit_two)
        g_vec[3:4, :width] += colsum(d_normed_two)
        g_vec[7:8, :width] += colsum(dy_s[...])
        g_vec[6:7, :width] += colsum(d_middle)
        d_branch = d_middle.astype(B16)
        g_out[...] += t_dot(mixed_s[...], d_branch)
        d_mixed = dot_t(d_branch, w_out[...]).astype(B16)
        for i in range(GROUP):
            dmix_s[i * deep : i * deep + rows] = d_mixed[i * rows : (i + 1) * rows]

        for i in range(GROUP):
            for pair in range(pairs):
                lanes = pl.ds(pair * LANES, LANES)
                q2 = qkv_s[pl.ds(i * deep, deep), lanes]
                k2 = qkv_s[pl.ds(i * deep, deep), pl.ds(width + pair * LANES, LANES)]
                v2 = qkv_s[pl.ds(i * deep, rows), pl.ds(2 * width + pair * LANES, LANES)]
                m2 = dmix_s[pl.ds(i * deep, deep), lanes]
                k_t = k2.T
                q_both, m_both = halves(q2), halves(m2)
                attends, slopes, parts = [], [], []
                for half in range(2):
                    attend = attend_s[i * 2 * pairs + 2 * pair + half]
                    probs = attend.astype(F32)
                    product = probs * dot_t(v2, m_both[half])
                    d_scores = product - probs * jnp.sum(product, axis=0, keepdims=True)
                    d_scores = d_scores.astype(B16)
                    attends.append(attend)
                    slopes.append(d_scores)
                    parts.append(
                        dot(
                            k_t[half * HEAD : (half + 1) * HEAD],
                            jnp.concatenate([d_scores, blank], axis=0),
                        )
                    )
                d_queries = (jnp.concatenate(parts, axis=0) * scale).T
                d_values = dot(jnp.concatenate(attends, axis=1), jnp.concatenate(m_both, axis=0))
                d_keys = dot(jnp.concatenate(slopes, axis=1), jnp.concatenate(q_both, axis=0))
                here = pl.ds(i * rows, rows)
                dj_s[here, lanes] = d_queries[:rows].astype(B16)
                dj_s[here, pl.ds(width + pair * LANES, LANES)] = d_keys.astype(B16)
                dj_s[here, pl.ds(2 * width + pair * LANES, LANES)] = d_values.astype(B16)

        g_vec[4:5, :width] += colsum(dj_s[:, :width].astype(F32))
        g_vec[5:6, :width] += colsum(dj_s[:, 2 * width :].astype(F32))
        g_qkv[...] += t_dot(normed_s[...], dj_s[...])
        d_normed = dot_t(dj_s[...], w_qkv[...])
        g_vec[0:1, :width] += colsum(d_normed * unit_one)
        g_vec[2:3, :width] += colsum(d_normed)
        d_input = d_middle + norm_back(d_normed, unit_one, factor_one, gain_one)
        for i in range(GROUP):
            gtok[0, i] = d_input[i * rows : i * rows + length].astype(B16)


def run_block(tokens, counts, cotangent, w_qkv, w_out, w_fc1, w_fc2, vec):
    micro, slots, length, width = tokens.shape
    hidden_units = w_fc1.shape[1]
    heads = width // HEAD
    rows = round_up(length, 16)
    deep = round_up(length, LANES)
    chunk = 512 if hidden_units % 512 == 0 else hidden_units

    def image_in(m, p, counts_ref):
        return (m, jnp.minimum(p, (counts_ref[m] - 1) // GROUP), 0, 0)

    def image_out(m, p, counts_ref):
        return (m, p, 0, 0)

    def whole(m, p, counts_ref):
        return (0, 0)

    block = (1, GROUP, length, width)
    weights = (w_qkv, w_out, w_fc1, w_fc2, vec)
    once = pl.Buffered(1)
    grads = [jax.ShapeDtypeStruct(w.shape, F32) for w in weights]
    return pl.pallas_call(
        functools.partial(block_kernel, length, chunk),
        grid_spec=pltpu.PrefetchScalarGridSpec(
            num_scalar_prefetch=1,
            grid=(micro, slots // GROUP),
            in_specs=[
                pl.BlockSpec(block, image_in),
                pl.BlockSpec(block, image_in),
                *[pl.BlockSpec(w.shape, whole, pipeline_mode=once) for w in weights],
            ],
            out_specs=[
                pl.BlockSpec(block, image_out),
                pl.BlockSpec(block, image_out),
                *[pl.BlockSpec(w.shape, whole) for w in weights],
            ],
            scratch_shapes=[
                pltpu.VMEM((GROUP * rows, width), F32),
                pltpu.VMEM((GROUP * rows, width), F32),
                pltpu.VMEM((GROUP * rows, width), B16),
                pltpu.VMEM((GROUP * deep, 3 * width), B16),
                pltpu.VMEM((GROUP * heads, rows, deep), B16),
                pltpu.VMEM((GROUP * rows, width), B16),
                pltpu.VMEM((GROUP * deep, width), B16),
                pltpu.VMEM((GROUP * rows, 3 * width), B16),
            ],
        ),
        out_shape=[
            jax.ShapeDtypeStruct(tokens.shape, B16),
            jax.ShapeDtypeStruct(tokens.shape, B16),
            *grads,
        ],
        compiler_params=pltpu.CompilerParams(vmem_limit_bytes=56 * 2**20),
    )(counts, tokens, cotangent, *weights)


def body(tokens, counts, cotangent, w_qkv, w_out, w_fc1, w_fc2, gains, shifts, biases):
    width = tokens.shape[-1]
    devices = lax.axis_size(AXES)
    hidden_units = w_fc1.shape[0] * devices // width
    gather = lambda piece: lax.all_gather(piece, AXES, axis=0, tiled=True)
    mat_qkv = gather(w_qkv).reshape(width, 3 * width)
    mat_out = gather(w_out).reshape(width, width)
    mat_fc1 = gather(w_fc1).reshape(width, hidden_units)
    mat_fc2 = gather(w_fc2).reshape(hidden_units, width)
    small = gather(jnp.concatenate([gains, shifts, biases])).astype(F32).reshape(devices, -1)
    cuts = [gains.shape[0], gains.shape[0] + shifts.shape[0]]
    gain_all, shift_all, bias_all = [p.reshape(-1) for p in jnp.split(small, cuts, axis=1)]
    edge = 3 * width + hidden_units
    narrow = [
        gain_all.reshape(2, width),
        shift_all.reshape(2, width),
        bias_all[: 3 * width].reshape(3, width),
        bias_all[edge:].reshape(1, width),
    ]
    vec = jnp.concatenate(
        [
            jnp.pad(jnp.concatenate(narrow, axis=0), ((0, 0), (0, hidden_units - width))),
            bias_all[3 * width : edge].reshape(1, hidden_units),
            jnp.zeros((7, hidden_units), F32),
        ],
        axis=0,
    )
    result, grad_tokens, g_qkv, g_out, g_fc1, g_fc2, g_vec = run_block(
        tokens, counts[0], cotangent, mat_qkv, mat_out, mat_fc1, mat_fc2, vec
    )
    scatter = lambda whole: lax.psum_scatter(whole, AXES, scatter_dimension=0, tiled=True)
    grad_gains = g_vec[0:2, :width].reshape(devices, -1)
    grad_shifts = g_vec[2:4, :width].reshape(devices, -1)
    grad_biases = jnp.concatenate(
        [g_vec[4:7, :width].reshape(-1), g_vec[8], g_vec[7, :width]]
    ).reshape(devices, -1)
    small = scatter(jnp.concatenate([grad_gains, grad_shifts, grad_biases], axis=1).reshape(-1))
    grad_gains, grad_shifts, grad_biases = jnp.split(small, cuts)
    return (
        result,
        grad_tokens,
        scatter(g_qkv.reshape(-1)),
        scatter(g_out.reshape(-1)),
        scatter(g_fc1.reshape(-1)),
        scatter(g_fc2.reshape(-1)),
        grad_gains,
        grad_shifts,
        grad_biases,
    )


def solution(mesh):
    return jax.shard_map(
        body,
        mesh=mesh,
        in_specs=(
            P(None, AXES, None, None),
            P(AXES, None),
            P(None, AXES, None, None),
            P(AXES),
            P(AXES),
            P(AXES),
            P(AXES),
            P(AXES),
            P(AXES),
            P(AXES),
        ),
        out_specs=(
            P(None, AXES, None, None),
            P(None, AXES, None, None),
            P(AXES),
            P(AXES),
            P(AXES),
            P(AXES),
            P(AXES),
            P(AXES),
            P(AXES),
        ),
        check_vma=False,
    )
```

```python
import functools

import jax
import jax.numpy as jnp
from jax import lax
from jax.experimental import pallas as pl
from jax.experimental.pallas import tpu as pltpu
from jax.sharding import PartitionSpec as P

HEAD = 64
EPS = 1e-06
F32 = jnp.float32
B16 = jnp.bfloat16
AXES = ("gx", "gy")
GROUP = 2
LANES = 128


def round_up(value, unit):
    return -(-value // unit) * unit


def dot(left, right):
    return jnp.dot(left, right, preferred_element_type=F32)


def dot_t(left, right):
    return lax.dot_general(left, right, (((1,), (1,)), ((), ())), preferred_element_type=F32)


def t_dot(left, right):
    return lax.dot_general(left, right, (((0,), (0,)), ((), ())), preferred_element_type=F32)


def norm_parts(values):
    center = values - jnp.mean(values, axis=-1, keepdims=True)
    factor = lax.rsqrt(jnp.mean(center * center, axis=-1, keepdims=True) + EPS)
    return center * factor, factor


def norm_back(incoming, unit, factor, gain):
    scaled = incoming * gain
    return factor * (
        scaled
        - jnp.mean(scaled, axis=-1, keepdims=True)
        - unit * jnp.mean(scaled * unit, axis=-1, keepdims=True)
    )


def colsum(values):
    return jnp.sum(values, axis=0, keepdims=True)


def gelu_both(hidden):
    size = jnp.abs(hidden)
    t = 1.0 / (1.0 + (0.3275911 * 0.5**0.5) * size)
    bell = jnp.exp(-0.5 * hidden * hidden)
    poly = t * (
        0.127414796
        + t * (-0.142248368 + t * (0.7107068705 + t * (-0.7265760135 + t * 0.5307027145)))
    )
    tail = poly * bell
    area = jnp.where(hidden >= 0, 1.0 - tail, tail)
    return hidden * area, area + hidden * (bell * 0.3989422804014327)


def put_rows(x_s, block, rows, length):
    for i in range(GROUP):
        x_s[i * rows : i * rows + length] = block[0, i].astype(F32)


def halves(two, first_half):
    zero = jnp.zeros_like(two)
    return jnp.where(first_half, two, zero), jnp.where(first_half, zero, two)


def lower_lanes():
    return lax.broadcasted_iota(jnp.int32, (1, LANES), 1) < HEAD


def attend_kernel(length, counts, tok, w_qkv, vec, qkv, attend, mixed, x_s):
    width = tok.shape[-1]
    rows = x_s.shape[0] // GROUP
    deep = qkv.shape[1] // GROUP
    pairs = width // LANES
    micro, place = pl.program_id(0), pl.program_id(1)

    @pl.when((micro == 0) & (place == 0))
    def _():
        x_s[...] = jnp.zeros_like(x_s)

    @pl.when(place * GROUP < counts[micro])
    def _():
        put_rows(x_s, tok, rows, length)
        unit, _ = norm_parts(x_s[...])
        normed = (unit * vec[0:1, :width] + vec[2:3, :width]).astype(B16)
        queries = ((dot(normed, w_qkv[:, :width]) + vec[4:5, :width]) * HEAD**-0.5).astype(B16)
        keys_all = dot(normed, w_qkv[:, width : 2 * width]).astype(B16)
        values_all = (dot(normed, w_qkv[:, 2 * width :]) + vec[5:6, :width]).astype(B16)
        for i in range(GROUP):
            for at, part in enumerate((queries, keys_all, values_all)):
                cols = slice(at * width, (at + 1) * width)
                qkv[0, i * deep : i * deep + rows, cols] = part[i * rows : (i + 1) * rows]
            qkv[0, i * deep + rows : (i + 1) * deep] = jnp.zeros((deep - rows, 3 * width), B16)

        first_half = lower_lanes()
        tail = rows - 16
        hide = jnp.where(
            lax.broadcasted_iota(jnp.int32, (16, 1), 0) + tail < length, 0.0, -1e30
        ).astype(F32)
        blank = jnp.zeros((deep - rows, deep), B16)
        for i in range(GROUP):
            for pair in range(pairs):
                lanes = pl.ds(pair * LANES, LANES)
                q2 = qkv[0, pl.ds(i * deep, deep), lanes]
                k2 = qkv[0, pl.ds(i * deep, rows), pl.ds(width + pair * LANES, LANES)]
                v2 = qkv[0, pl.ds(i * deep, deep), pl.ds(2 * width + pair * LANES, LANES)]
                v_t = v2.T
                parts = []
                for half, q_one in enumerate(halves(q2, first_half)):
                    scores = dot_t(k2, q_one)
                    scores = jnp.concatenate([scores[:tail], scores[tail:] + hide], axis=0)
                    scores = jnp.exp(scores - jnp.max(scores, axis=0, keepdims=True))
                    total = jnp.sum(scores, axis=0, keepdims=True)
                    weights = (scores * (1.0 / total)).astype(B16)
                    attend[0, i * 2 * pairs + 2 * pair + half] = weights
                    mine = v_t[half * HEAD : (half + 1) * HEAD]
                    parts.append(dot(mine, jnp.concatenate([weights, blank], axis=0)))
                mixed_two = jnp.concatenate(parts, axis=0).T
                mixed[0, pl.ds(i * rows, rows), lanes] = mixed_two[:rows].astype(B16)


def feed_kernel(
    length, chunk, counts, tok, cot, mixed, w_out, w_fc1, w_fc2, vec,
    res, d_middle_out, d_mixed_out, o_out, o_fc1, o_fc2, g_vec, x_s, dy_s, g_out, g_fc1, g_fc2,
):
    width = tok.shape[-1]
    hidden_units = w_fc1.shape[1]
    rows = x_s.shape[0] // GROUP
    deep = d_mixed_out.shape[1] // GROUP
    micro, place = pl.program_id(0), pl.program_id(1)
    live_count = counts[micro]

    @pl.when((micro == 0) & (place == 0))
    def _():
        for ref in (x_s, dy_s, g_out, g_fc1, g_fc2, g_vec):
            ref[...] = jnp.zeros_like(ref)

    @pl.when(place * GROUP >= live_count)
    def _():
        res[...] = jnp.zeros_like(res)

    @pl.when(place * GROUP < live_count)
    def _():
        put_rows(x_s, tok, rows, length)
        for i in range(GROUP):
            live = (place * GROUP + i < live_count).astype(F32)
            dy_s[i * rows : i * rows + length] = cot[0, i].astype(F32) * live
        gain, shift = vec[1:2, :width], vec[3:4, :width]
        middle = x_s[...] + dot(mixed[0], w_out[...]) + vec[6:7, :width]
        unit, factor = norm_parts(middle)
        normed = (unit * gain + shift).astype(B16)
        d_last = dy_s[...].astype(B16)
        last = vec[7:8, :width]
        d_normed = 0.0
        for at in range(0, hidden_units, chunk):
            cols = slice(at, at + chunk)
            hidden = dot(normed, w_fc1[:, cols]) + vec[8:9, cols]
            active, slope = gelu_both(hidden)
            active = active.astype(B16)
            last = last + dot(active, w_fc2[cols, :])
            d_hidden = dot_t(d_last, w_fc2[cols, :]) * slope
            g_vec[8:9, cols] += colsum(d_hidden)
            d_hidden = d_hidden.astype(B16)
            d_normed = d_normed + dot_t(d_hidden, w_fc1[:, cols])
            g_fc2[cols, :] += t_dot(active, d_last)
            g_fc1[:, cols] += t_dot(normed, d_hidden)
        result = middle + last
        for i in range(GROUP):
            live = (place * GROUP + i < live_count).astype(F32)
            res[0, i] = (result[i * rows : i * rows + length] * live).astype(B16)
        d_middle = dy_s[...] + norm_back(d_normed, unit, factor, gain)
        d_middle_out[0] = d_middle
        g_vec[1:2, :width] += colsum(d_normed * unit)
        g_vec[3:4, :width] += colsum(d_normed)
        g_vec[7:8, :width] += colsum(dy_s[...])
        g_vec[6:7, :width] += colsum(d_middle)
        d_branch = d_middle.astype(B16)
        g_out[...] += t_dot(mixed[0], d_branch)
        d_mixed = dot_t(d_branch, w_out[...]).astype(B16)
        for i in range(GROUP):
            d_mixed_out[0, i * deep : i * deep + rows] = d_mixed[i * rows : (i + 1) * rows]
            d_mixed_out[0, i * deep + rows : (i + 1) * deep] = jnp.zeros(
                (deep - rows, width), B16
            )

    @pl.when(last_step())
    def _():
        for whole, total in ((o_out, g_out), (o_fc1, g_fc1), (o_fc2, g_fc2)):
            whole[...] = total[...].astype(B16)


def last_step():
    return (pl.program_id(0) == pl.num_programs(0) - 1) & (
        pl.program_id(1) == pl.num_programs(1) - 1
    )


def back_kernel(
    length, counts, tok, qkv, attend, d_mixed, d_middle, w_qkv, vec, gtok, o_qkv, g_vec, x_s, dj_s, g_qkv
):
    width = tok.shape[-1]
    rows = x_s.shape[0] // GROUP
    deep = qkv.shape[1] // GROUP
    pairs = width // LANES
    micro, place = pl.program_id(0), pl.program_id(1)

    @pl.when((micro == 0) & (place == 0))
    def _():
        for ref in (x_s, g_qkv, g_vec):
            ref[...] = jnp.zeros_like(ref)

    @pl.when(place * GROUP >= counts[micro])
    def _():
        gtok[...] = jnp.zeros_like(gtok)

    @pl.when(place * GROUP < counts[micro])
    def _():
        put_rows(x_s, tok, rows, length)
        first_half = lower_lanes()
        blank = jnp.zeros((deep - rows, deep), B16)
        for i in range(GROUP):
            for pair in range(pairs):
                lanes = pl.ds(pair * LANES, LANES)
                key_lanes = pl.ds(width + pair * LANES, LANES)
                value_lanes = pl.ds(2 * width + pair * LANES, LANES)
                q2 = qkv[0, pl.ds(i * deep, deep), lanes]
                k2 = qkv[0, pl.ds(i * deep, deep), key_lanes]
                v2 = qkv[0, pl.ds(i * deep, rows), value_lanes]
                m2 = d_mixed[0, pl.ds(i * deep, deep), lanes]
                k_t = k2.T
                q_both, m_both = halves(q2, first_half), halves(m2, first_half)
                attends, slopes, parts = [], [], []
                for half in range(2):
                    weights = attend[0, i * 2 * pairs + 2 * pair + half]
                    probs = weights.astype(F32)
                    product = probs * dot_t(v2, m_both[half])
                    d_scores = product - probs * jnp.sum(product, axis=0, keepdims=True)
                    d_scores = d_scores.astype(B16)
                    attends.append(weights)
                    slopes.append(d_scores)
                    mine = k_t[half * HEAD : (half + 1) * HEAD]
                    parts.append(dot(mine, jnp.concatenate([d_scores, blank], axis=0)))
                d_queries = (jnp.concatenate(parts, axis=0) * HEAD**-0.5).T
                d_values = dot(jnp.concatenate(attends, axis=1), jnp.concatenate(m_both, axis=0))
                d_keys = dot(jnp.concatenate(slopes, axis=1), jnp.concatenate(q_both, axis=0))
                here = pl.ds(i * rows, rows)
                dj_s[here, lanes] = d_queries[:rows].astype(B16)
                dj_s[here, key_lanes] = d_keys.astype(B16)
                dj_s[here, value_lanes] = d_values.astype(B16)

        gain = vec[0:1, :width]
        unit, factor = norm_parts(x_s[...])
        normed = (unit * gain + vec[2:3, :width]).astype(B16)
        g_vec[4:5, :width] += colsum(dj_s[:, :width].astype(F32))
        g_vec[5:6, :width] += colsum(dj_s[:, 2 * width :].astype(F32))
        g_qkv[...] += t_dot(normed, dj_s[...])
        d_normed = dot_t(dj_s[...], w_qkv[...])
        g_vec[0:1, :width] += colsum(d_normed * unit)
        g_vec[2:3, :width] += colsum(d_normed)
        d_input = d_middle[0] + norm_back(d_normed, unit, factor, gain)
        for i in range(GROUP):
            gtok[0, i] = d_input[i * rows : i * rows + length].astype(B16)

    @pl.when(last_step())
    def _():
        o_qkv[...] = g_qkv[...].astype(B16)


def run_pairs(kernel, tokens, counts, inputs, outputs, scratch, flops):
    micro, slots, length, width = tokens.shape
    places = slots // GROUP

    def near(m, p, c):
        return jnp.minimum(p, (c[m] - 1) // GROUP)

    def spec(kind, shape, out):
        if kind == "image":
            block = (1, GROUP, length, width)
            if out:
                return pl.BlockSpec(block, lambda m, p, c: (m, p, 0, 0))
            return pl.BlockSpec(block, lambda m, p, c: (m, near(m, p, c), 0, 0))
        if kind == "pair":
            rest = len(shape) - 1
            return pl.BlockSpec(
                (1, *shape[1:]), lambda m, p, c: (m * places + near(m, p, c),) + (0,) * rest
            )
        once = {} if out else {"pipeline_mode": pl.Buffered(1)}
        return pl.BlockSpec(shape, lambda m, p, c: (0,) * len(shape), **once)

    return pl.pallas_call(
        kernel,
        grid_spec=pltpu.PrefetchScalarGridSpec(
            num_scalar_prefetch=1,
            grid=(micro, places),
            in_specs=[spec(kind, a.shape, False) for kind, a in inputs],
            out_specs=[spec(kind, a.shape, True) for kind, a in outputs],
            scratch_shapes=scratch,
        ),
        out_shape=[a for _, a in outputs],
        cost_estimate=pl.CostEstimate(
            flops=flops, bytes_accessed=64 * 2**20, transcendentals=0
        ),
        compiler_params=pltpu.CompilerParams(vmem_limit_bytes=56 * 2**20),
    )(counts, *[a for _, a in inputs])


def groups():
    slow, fast = lax.axis_size("gx"), lax.axis_size("gy")
    cores = 2 if slow % 2 == 0 else 1
    return slow // cores, cores, fast


def part_of(part):
    sizes = groups()
    step = 1
    for size in sizes[part + 1 :]:
        step *= size
    return step, sizes[part], (lax.axis_index(AXES) // step) % sizes[part]


def swap(value, step):
    devices = lax.axis_size(AXES)
    return lax.ppermute(value, AXES, [(i, i ^ step) for i in range(devices)])


def send_whole(value, part):
    step, size, _ = part_of(part)
    return [value] + [swap(value, step * k) for k in range(1, size)]


def join(got, part, axis):
    _, size, at = part_of(part)
    shape = got[0].shape[:axis] + (size,) + got[0].shape[axis:]
    whole = jnp.zeros(shape, got[0].dtype)
    for k in range(size):
        whole = lax.dynamic_update_index_in_dim(whole, got[k], at ^ k, axis)
    return whole


def gather(value, part, axis):
    return join(send_whole(value, part), part, axis)


def cut(value, part, axis):
    _, size, at = part_of(part)
    value = value.astype(B16)
    return [lax.dynamic_index_in_dim(value, at ^ k, axis, keepdims=False) for k in range(size)]


def send_cut(blocks, part):
    step, _, _ = part_of(part)
    return blocks[:1] + [swap(block, step * k) for k, block in enumerate(blocks) if k]


def add_up(got):
    total = got[0].astype(F32)
    for block in got[1:]:
        total = total + block.astype(F32)
    return total


def scatter(value, part, axis):
    return add_up(send_cut(cut(value, part, axis), part))


def lanes_of(value, lead):
    fill = -value.shape[-1] % LANES
    if fill:
        value = jnp.pad(value, [(0, 0)] * (value.ndim - 1) + [(0, fill)])
    return value.reshape(lead + (-1, LANES))


def body(tokens, counts, cotangent, w_qkv, w_out, w_fc1, w_fc2, gains, shifts, biases):
    micro, slots, length, width = tokens.shape
    devices = lax.axis_size(AXES)
    hidden_units = w_fc1.shape[0] * devices // width
    heads = width // HEAD
    rows = round_up(length, 16)
    deep = round_up(length, LANES)
    chunk = 512 if hidden_units % 512 == 0 else hidden_units
    pairs = micro * slots // GROUP
    n_small = gains.shape[0] + shifts.shape[0] + biases.shape[0]
    cuts = [gains.shape[0], gains.shape[0] + shifts.shape[0]]

    small = jnp.concatenate([gains, shifts, biases])
    shards = [lanes_of(w, ()) for w in (w_qkv, small)]
    n_qkv = shards[0].shape[0]
    first = gather(jnp.concatenate(shards), 0, 0)
    shards = [lanes_of(w, ()) for w in (w_out, w_fc1, w_fc2)]
    n_rest = [w.shape[0] for w in shards]
    rest = gather(jnp.concatenate(shards), 0, 0)
    first = gather(gather(first, 2, 1), 1, 1)
    rest = gather(rest, 1, 1)
    first, rest = lax.optimization_barrier((first, rest))
    first = first.reshape((devices,) + first.shape[3:])
    rest = send_whole(rest, 2)

    def matrix(part, size, shape):
        return part.reshape(devices, -1)[:, :size].reshape(shape)

    mat_qkv = matrix(first[:, :n_qkv], w_qkv.shape[0], (width, 3 * width))
    small = first[:, n_qkv:].reshape(devices, -1)[:, :n_small].astype(F32)
    gain_all, shift_all, bias_all = [p.reshape(-1) for p in jnp.split(small, cuts, axis=1)]
    edge = 3 * width + hidden_units
    narrow = [
        gain_all.reshape(2, width),
        shift_all.reshape(2, width),
        bias_all[: 3 * width].reshape(3, width),
        bias_all[edge:].reshape(1, width),
    ]
    vec = jnp.concatenate(
        [
            jnp.pad(jnp.concatenate(narrow, axis=0), ((0, 0), (0, hidden_units - width))),
            bias_all[3 * width : edge].reshape(1, hidden_units),
            jnp.zeros((7, hidden_units), F32),
        ],
        axis=0,
    )

    of = jax.ShapeDtypeStruct
    image = of(tokens.shape, B16)
    counts = counts[0]
    rows_f32 = pltpu.VMEM((GROUP * rows, width), F32)
    tokens_here = micro * slots * length
    qkv, attend, mixed = run_pairs(
        functools.partial(attend_kernel, length),
        tokens,
        counts,
        [("image", tokens), ("whole", mat_qkv), ("whole", vec)],
        [
            ("pair", of((pairs, GROUP * deep, 3 * width), B16)),
            ("pair", of((pairs, GROUP * heads, rows, deep), B16)),
            ("pair", of((pairs, GROUP * rows, width), B16)),
        ],
        [rows_f32],
        tokens_here * (6 * width * width + 4 * length * width),
    )
    mixed, rest = lax.optimization_barrier((mixed, rest))
    rest = join(rest, 2, 2)
    rest = rest.reshape((devices,) + rest.shape[3:])
    cut_out, cut_fc1 = n_rest[0], n_rest[0] + n_rest[1]
    mat_out = matrix(rest[:, :cut_out], w_out.shape[0], (width, width))
    mat_fc1 = matrix(rest[:, cut_out:cut_fc1], w_fc1.shape[0], (width, hidden_units))
    mat_fc2 = matrix(rest[:, cut_fc1:], w_fc2.shape[0], (hidden_units, width))
    result, d_middle, d_mixed, g_out, g_fc1, g_fc2, g_vec_b = run_pairs(
        functools.partial(feed_kernel, length, chunk),
        tokens,
        counts,
        [
            ("image", tokens),
            ("image", cotangent),
            ("pair", mixed),
            ("whole", mat_out),
            ("whole", mat_fc1),
            ("whole", mat_fc2),
            ("whole", vec),
        ],
        [
            ("image", image),
            ("pair", of((pairs, GROUP * rows, width), F32)),
            ("pair", of((pairs, GROUP * deep, width), B16)),
            ("whole", of(mat_out.shape, B16)),
            ("whole", of(mat_fc1.shape, B16)),
            ("whole", of(mat_fc2.shape, B16)),
            ("whole", of(vec.shape, F32)),
        ],
        [rows_f32, rows_f32, *[pltpu.VMEM(m.shape, F32) for m in (mat_out, mat_fc1, mat_fc2)]],
        tokens_here * 6 * width * (width + 2 * hidden_units),
    )
    flat = lambda whole: whole.reshape(devices, -1)
    lead = (devices,)
    parts = [lanes_of(flat(g), lead) for g in (g_out, g_fc1, g_fc2)]
    rest = jnp.concatenate(parts, axis=1)
    rest = cut(rest.reshape(groups() + rest.shape[1:]), 2, 2)
    d_mixed, rest = lax.optimization_barrier((d_mixed, rest))
    rest = send_cut(rest, 2)
    grad_tokens, g_qkv, g_vec_c = run_pairs(
        functools.partial(back_kernel, length),
        tokens,
        counts,
        [
            ("image", tokens),
            ("pair", qkv),
            ("pair", attend),
            ("pair", d_mixed),
            ("pair", d_middle),
            ("whole", mat_qkv),
            ("whole", vec),
        ],
        [("image", image), ("whole", of(mat_qkv.shape, B16)), ("whole", of(vec.shape, F32))],
        [
            rows_f32,
            pltpu.VMEM((GROUP * rows, 3 * width), B16),
            pltpu.VMEM(mat_qkv.shape, F32),
        ],
        tokens_here * (12 * width * width + 8 * length * width),
    )
    g_qkv, rest = lax.optimization_barrier((g_qkv, rest))
    g_vec = g_vec_b + g_vec_c
    grad_biases = jnp.concatenate(
        [g_vec[4:7, :width].reshape(-1), g_vec[8], g_vec[7, :width]]
    )
    small = jnp.concatenate(
        [flat(g_vec[0:2, :width]), flat(g_vec[2:4, :width]), flat(grad_biases)], axis=1
    )
    parts = [lanes_of(flat(g_qkv), lead), lanes_of(small.astype(B16), lead)]
    first = jnp.concatenate(parts, axis=1)
    first = scatter(first.reshape(groups() + first.shape[1:]), 1, 1)
    rest = scatter(add_up(rest), 1, 1)
    first = scatter(first, 2, 1)
    rest = scatter(rest, 0, 0)
    first = scatter(first, 0, 0)
    grad_qkv = first[:n_qkv].reshape(-1)[: w_qkv.shape[0]]
    grad_gains, grad_shifts, grad_biases = jnp.split(first[n_qkv:].reshape(-1)[:n_small], cuts)
    return (
        result,
        grad_tokens,
        grad_qkv,
        rest[:cut_out].reshape(-1)[: w_out.shape[0]],
        rest[cut_out:cut_fc1].reshape(-1)[: w_fc1.shape[0]],
        rest[cut_fc1:].reshape(-1)[: w_fc2.shape[0]],
        grad_gains,
        grad_shifts,
        grad_biases,
    )


def solution(mesh):
    return jax.shard_map(
        body,
        mesh=mesh,
        in_specs=(
            P(None, AXES, None, None),
            P(AXES, None),
            P(None, AXES, None, None),
            P(AXES),
            P(AXES),
            P(AXES),
            P(AXES),
            P(AXES),
            P(AXES),
            P(AXES),
        ),
        out_specs=(
            P(None, AXES, None, None),
            P(None, AXES, None, None),
            P(AXES),
            P(AXES),
            P(AXES),
            P(AXES),
            P(AXES),
            P(AXES),
            P(AXES),
        ),
        check_vma=False,
    )
```

```python
import functools

import jax
import jax.numpy as jnp
from jax import lax
from jax.experimental import pallas as pl
from jax.experimental.pallas import tpu as pltpu
from jax.sharding import PartitionSpec as P

HEAD = 64
EPS = 1e-06
F32 = jnp.float32
B16 = jnp.bfloat16
AXES = ("gx", "gy")
GROUP = 2
LANES = 128
OF = jax.ShapeDtypeStruct


def round_up(value, unit):
    return -(-value // unit) * unit


def dot(left, right):
    return jnp.dot(left, right, preferred_element_type=F32)


def dot_t(left, right):
    return lax.dot_general(left, right, (((1,), (1,)), ((), ())), preferred_element_type=F32)


def t_dot(left, right):
    return lax.dot_general(left, right, (((0,), (0,)), ((), ())), preferred_element_type=F32)


def norm_parts(values):
    center = values - jnp.mean(values, axis=-1, keepdims=True)
    factor = lax.rsqrt(jnp.mean(center * center, axis=-1, keepdims=True) + EPS)
    return center * factor, factor


def norm_back(incoming, unit, factor, gain):
    scaled = incoming * gain
    return factor * (
        scaled
        - jnp.mean(scaled, axis=-1, keepdims=True)
        - unit * jnp.mean(scaled * unit, axis=-1, keepdims=True)
    )


def colsum(values):
    return jnp.sum(values, axis=0, keepdims=True)


def gelu_both(hidden):
    size = jnp.abs(hidden)
    t = 1.0 / (1.0 + (0.3275911 * 0.5**0.5) * size)
    bell = jnp.exp(-0.5 * hidden * hidden)
    poly = t * (
        0.127414796
        + t * (-0.142248368 + t * (0.7107068705 + t * (-0.7265760135 + t * 0.5307027145)))
    )
    tail = poly * bell
    area = jnp.where(hidden >= 0, 1.0 - tail, tail)
    return hidden * area, area + hidden * (bell * 0.3989422804014327)


def put_rows(x_s, block, rows, length):
    for i in range(GROUP):
        x_s[i * rows : i * rows + length] = block[0, i].astype(F32)


def halves(two, first_half):
    zero = jnp.zeros_like(two)
    return jnp.where(first_half, two, zero), jnp.where(first_half, zero, two)


def lower_lanes():
    return lax.broadcasted_iota(jnp.int32, (1, LANES), 1) < HEAD


def attend_kernel(length, counts, tok, w_qkv, vec, qkv, attend, mixed, x_s):
    width = tok.shape[-1]
    rows = x_s.shape[0] // GROUP
    deep = qkv.shape[1] // GROUP
    pairs = width // LANES
    micro, place = pl.program_id(0), pl.program_id(1)

    @pl.when((micro == 0) & (place == 0))
    def _():
        x_s[...] = jnp.zeros_like(x_s)

    @pl.when(place * GROUP < counts[micro])
    def _():
        put_rows(x_s, tok, rows, length)
        unit, _ = norm_parts(x_s[...])
        normed = (unit * vec[0:1, :width] + vec[2:3, :width]).astype(B16)
        queries = ((dot(normed, w_qkv[:, :width]) + vec[4:5, :width]) * HEAD**-0.5).astype(B16)
        keys_all = dot(normed, w_qkv[:, width : 2 * width]).astype(B16)
        values_all = (dot(normed, w_qkv[:, 2 * width :]) + vec[5:6, :width]).astype(B16)
        for i in range(GROUP):
            for at, part in enumerate((queries, keys_all, values_all)):
                cols = slice(at * width, (at + 1) * width)
                qkv[0, i * deep : i * deep + rows, cols] = part[i * rows : (i + 1) * rows]
            qkv[0, i * deep + rows : (i + 1) * deep] = jnp.zeros((deep - rows, 3 * width), B16)

        first_half = lower_lanes()
        tail = rows - 16
        hide = jnp.where(
            lax.broadcasted_iota(jnp.int32, (16, 1), 0) + tail < length, 0.0, -1e30
        ).astype(F32)
        blank = jnp.zeros((deep - rows, deep), B16)
        todo = [(i, pair) for i in range(GROUP) for pair in range(pairs)]

        def start(i, pair):
            q2 = qkv[0, pl.ds(i * deep, deep), pl.ds(pair * LANES, LANES)]
            k2 = qkv[0, pl.ds(i * deep, rows), pl.ds(width + pair * LANES, LANES)]
            return [dot_t(k2, q_one) for q_one in halves(q2, first_half)]

        def soften(i, pair, both):
            for half, scores in enumerate(both):
                scores = jnp.concatenate([scores[:tail], scores[tail:] + hide], axis=0)
                scores = jnp.exp(scores - jnp.max(scores, axis=0, keepdims=True))
                total = jnp.sum(scores, axis=0, keepdims=True)
                attend[0, i * 2 * pairs + 2 * pair + half] = (scores * (1.0 / total)).astype(B16)

        def mix(i, pair):
            v_t = qkv[0, pl.ds(i * deep, deep), pl.ds(2 * width + pair * LANES, LANES)].T
            parts = []
            for half in range(2):
                weights = attend[0, i * 2 * pairs + 2 * pair + half]
                mine = v_t[half * HEAD : (half + 1) * HEAD]
                parts.append(dot(mine, jnp.concatenate([weights, blank], axis=0)))
            mixed_two = jnp.concatenate(parts, axis=0).T
            mixed[0, pl.ds(i * rows, rows), pl.ds(pair * LANES, LANES)] = mixed_two[:rows].astype(B16)

        both = start(*todo[0])
        for at, here in enumerate(todo):
            after = start(*todo[at + 1]) if at + 1 < len(todo) else None
            soften(*here, both)
            if at:
                mix(*todo[at - 1])
            both = after
        mix(*todo[-1])


def feed_kernel(
    length, chunk, counts, tok, cot, mixed, w_out, w_fc1, w_fc2, vec,
    res, d_middle_out, d_mixed_out, o_out, o_fc1, o_fc2, g_vec, x_s, dy_s, g_out, g_fc1, g_fc2,
):
    width = tok.shape[-1]
    hidden_units = w_fc1.shape[1]
    rows = x_s.shape[0] // GROUP
    deep = d_mixed_out.shape[1] // GROUP
    micro, place = pl.program_id(0), pl.program_id(1)
    live_count = counts[micro]

    @pl.when((micro == 0) & (place == 0))
    def _():
        for ref in (x_s, dy_s, g_out, g_fc1, g_fc2, g_vec):
            ref[...] = jnp.zeros_like(ref)

    @pl.when(place * GROUP >= live_count)
    def _():
        res[...] = jnp.zeros_like(res)

    @pl.when(place * GROUP < live_count)
    def _():
        put_rows(x_s, tok, rows, length)
        for i in range(GROUP):
            live = (place * GROUP + i < live_count).astype(F32)
            dy_s[i * rows : i * rows + length] = cot[0, i].astype(F32) * live
        gain, shift = vec[1:2, :width], vec[3:4, :width]
        middle = x_s[...] + dot(mixed[0], w_out[...]) + vec[6:7, :width]
        unit, factor = norm_parts(middle)
        normed = (unit * gain + shift).astype(B16)
        d_last = dy_s[...].astype(B16)
        last = vec[7:8, :width]
        d_normed = 0.0
        d_last_t, normed_t = d_last.T, normed.T
        starts = list(range(0, hidden_units, chunk))
        ahead, held = None, None
        for at in starts + [None] + [None]:
            if at is not None:
                cols = slice(at, at + chunk)
                hidden = dot(normed, w_fc1[:, cols]) + vec[8:9, cols]
                d_active = dot_t(d_last, w_fc2[cols, :])
            if held is not None:
                old, active_old, d_hidden_old = held
                last = last + dot(active_old, w_fc2[old, :])
                d_normed = d_normed + dot_t(d_hidden_old, w_fc1[:, old])
                g_fc2[:, old] += dot(d_last_t, active_old)
                g_fc1[:, old] += dot(normed_t, d_hidden_old)
                held = None
            if ahead is not None:
                now, hidden_now, d_active_now = ahead
                active, slope = gelu_both(hidden_now)
                active = active.astype(B16)
                d_hidden = d_active_now * slope
                g_vec[8:9, now] += colsum(d_hidden)
                d_hidden = d_hidden.astype(B16)
                held = (now, active, d_hidden)
            ahead = (cols, hidden, d_active) if at is not None else None
        result = middle + last
        for i in range(GROUP):
            live = (place * GROUP + i < live_count).astype(F32)
            res[0, i] = (result[i * rows : i * rows + length] * live).astype(B16)
        d_middle = dy_s[...] + norm_back(d_normed, unit, factor, gain)
        d_middle_out[0] = d_middle
        g_vec[1:2, :width] += colsum(d_normed * unit)
        g_vec[3:4, :width] += colsum(d_normed)
        g_vec[7:8, :width] += colsum(dy_s[...])
        g_vec[6:7, :width] += colsum(d_middle)
        d_branch = d_middle.astype(B16)
        g_out[...] += t_dot(mixed[0], d_branch)
        d_mixed = dot_t(d_branch, w_out[...]).astype(B16)
        for i in range(GROUP):
            d_mixed_out[0, i * deep : i * deep + rows] = d_mixed[i * rows : (i + 1) * rows]
            d_mixed_out[0, i * deep + rows : (i + 1) * deep] = jnp.zeros(
                (deep - rows, width), B16
            )

    @pl.when(last_step())
    def _():
        o_out[...] = g_out[...].astype(B16)
        o_fc1[...] = g_fc1[...].astype(B16)
        for at in range(0, hidden_units, width):
            o_fc2[at : at + width] = g_fc2[:, at : at + width].T.astype(B16)


def last_step():
    return (pl.program_id(0) == pl.num_programs(0) - 1) & (
        pl.program_id(1) == pl.num_programs(1) - 1
    )


def back_kernel(
    length, counts, tok, qkv, attend, d_mixed, d_middle, w_qkv, vec, gtok, o_qkv, g_vec, x_s, dj_s, g_qkv
):
    width = tok.shape[-1]
    rows = x_s.shape[0] // GROUP
    deep = qkv.shape[1] // GROUP
    pairs = width // LANES
    micro, place = pl.program_id(0), pl.program_id(1)

    @pl.when((micro == 0) & (place == 0))
    def _():
        for ref in (x_s, g_qkv, g_vec):
            ref[...] = jnp.zeros_like(ref)

    @pl.when(place * GROUP >= counts[micro])
    def _():
        gtok[...] = jnp.zeros_like(gtok)

    @pl.when(place * GROUP < counts[micro])
    def _():
        put_rows(x_s, tok, rows, length)
        first_half = lower_lanes()
        blank = jnp.zeros((deep - rows, deep), B16)
        todo = [(i, pair) for i in range(GROUP) for pair in range(pairs)]

        def lanes_at(part, pair):
            return pl.ds(part * width + pair * LANES, LANES)

        def start(i, pair):
            v2 = qkv[0, pl.ds(i * deep, rows), lanes_at(2, pair)]
            m2 = d_mixed[0, pl.ds(i * deep, deep), lanes_at(0, pair)]
            return [dot_t(v2, m_one) for m_one in halves(m2, first_half)]

        def soften(i, pair, both):
            slopes = []
            for half, d_attend in enumerate(both):
                probs = attend[0, i * 2 * pairs + 2 * pair + half].astype(F32)
                product = probs * d_attend
                d_scores = product - probs * jnp.sum(product, axis=0, keepdims=True)
                slopes.append(d_scores.astype(B16))
            return slopes

        def finish(i, pair, slopes):
            q2 = qkv[0, pl.ds(i * deep, deep), lanes_at(0, pair)]
            k_t = qkv[0, pl.ds(i * deep, deep), lanes_at(1, pair)].T
            m2 = d_mixed[0, pl.ds(i * deep, deep), lanes_at(0, pair)]
            q_both, m_both = halves(q2, first_half), halves(m2, first_half)
            parts = [
                dot(
                    k_t[half * HEAD : (half + 1) * HEAD],
                    jnp.concatenate([slopes[half], blank], axis=0),
                )
                for half in range(2)
            ]
            attends = [attend[0, i * 2 * pairs + 2 * pair + half] for half in range(2)]
            d_queries = (jnp.concatenate(parts, axis=0) * HEAD**-0.5).T
            d_values = dot(jnp.concatenate(attends, axis=1), jnp.concatenate(m_both, axis=0))
            d_keys = dot(jnp.concatenate(slopes, axis=1), jnp.concatenate(q_both, axis=0))
            here = pl.ds(i * rows, rows)
            dj_s[here, lanes_at(0, pair)] = d_queries[:rows].astype(B16)
            dj_s[here, lanes_at(1, pair)] = d_keys.astype(B16)
            dj_s[here, lanes_at(2, pair)] = d_values.astype(B16)

        both, slopes = start(*todo[0]), None
        for at, here in enumerate(todo):
            after = start(*todo[at + 1]) if at + 1 < len(todo) else None
            if at:
                finish(*todo[at - 1], slopes)
            slopes = soften(*here, both)
            both = after
        finish(*todo[-1], slopes)

        gain = vec[0:1, :width]
        unit, factor = norm_parts(x_s[...])
        normed = (unit * gain + vec[2:3, :width]).astype(B16)
        g_vec[4:5, :width] += colsum(dj_s[:, :width].astype(F32))
        g_vec[5:6, :width] += colsum(dj_s[:, 2 * width :].astype(F32))
        g_qkv[...] += t_dot(normed, dj_s[...])
        d_normed = dot_t(dj_s[...], w_qkv[...])
        g_vec[0:1, :width] += colsum(d_normed * unit)
        g_vec[2:3, :width] += colsum(d_normed)
        d_input = d_middle[0] + norm_back(d_normed, unit, factor, gain)
        for i in range(GROUP):
            gtok[0, i] = d_input[i * rows : i * rows + length].astype(B16)

    @pl.when(last_step())
    def _():
        o_qkv[...] = g_qkv[...].astype(B16)


def run_pairs(kernel, tokens, counts, inputs, outputs, scratch, flops):
    micro, slots, length, width = tokens.shape
    places = slots // GROUP

    def near(m, p, c):
        return jnp.minimum(p, (c[m] - 1) // GROUP)

    def spec(kind, shape, out):
        if kind == "image":
            block = (1, GROUP, length, width)
            if out:
                return pl.BlockSpec(block, lambda m, p, c: (m, p, 0, 0))
            return pl.BlockSpec(block, lambda m, p, c: (m, near(m, p, c), 0, 0))
        if kind == "pair":
            rest = len(shape) - 1
            return pl.BlockSpec(
                (1, *shape[1:]), lambda m, p, c: (m * places + near(m, p, c),) + (0,) * rest
            )
        once = {} if out else {"pipeline_mode": pl.Buffered(1)}
        return pl.BlockSpec(shape, lambda m, p, c: (0,) * len(shape), **once)

    return pl.pallas_call(
        kernel,
        grid_spec=pltpu.PrefetchScalarGridSpec(
            num_scalar_prefetch=1,
            grid=(micro, places),
            in_specs=[spec(kind, a.shape, False) for kind, a in inputs],
            out_specs=[spec(kind, a.shape, True) for kind, a in outputs],
            scratch_shapes=scratch,
        ),
        out_shape=[a for _, a in outputs],
        cost_estimate=pl.CostEstimate(
            flops=flops, bytes_accessed=64 * 2**20, transcendentals=0
        ),
        compiler_params=pltpu.CompilerParams(vmem_limit_bytes=56 * 2**20),
    )(counts, *[a for _, a in inputs])


def sizes_of(tokens):
    micro, slots, length, width = tokens.shape
    rows, deep = round_up(length, 16), round_up(length, LANES)
    return micro * slots // GROUP, rows, deep, length, width, micro * slots * length


def run_attend(tokens, counts, mat_qkv, vec):
    pairs, rows, deep, length, width, total = sizes_of(tokens)
    heads = width // HEAD
    return run_pairs(
        functools.partial(attend_kernel, length),
        tokens,
        counts,
        [("image", tokens), ("whole", mat_qkv), ("whole", vec)],
        [
            ("pair", OF((pairs, GROUP * deep, 3 * width), B16)),
            ("pair", OF((pairs, GROUP * heads, rows, deep), B16)),
            ("pair", OF((pairs, GROUP * rows, width), B16)),
        ],
        [pltpu.VMEM((GROUP * rows, width), F32)],
        total * (6 * width * width + 4 * length * width),
    )


def run_feed(tokens, counts, cotangent, mixed, mat_out, mat_fc1, mat_fc2, vec):
    pairs, rows, deep, length, width, total = sizes_of(tokens)
    hidden_units = mat_fc1.shape[1]
    chunk = 256 if hidden_units % 256 == 0 else hidden_units
    matrices = (mat_out, mat_fc1, mat_fc2)
    return run_pairs(
        functools.partial(feed_kernel, length, chunk),
        tokens,
        counts,
        [
            ("image", tokens),
            ("image", cotangent),
            ("pair", mixed),
            *[("whole", m) for m in matrices],
            ("whole", vec),
        ],
        [
            ("image", OF(tokens.shape, B16)),
            ("pair", OF((pairs, GROUP * rows, width), F32)),
            ("pair", OF((pairs, GROUP * deep, width), B16)),
            *[("whole", OF(m.shape, B16)) for m in matrices],
            ("whole", OF(vec.shape, F32)),
        ],
        [
            pltpu.VMEM((GROUP * rows, width), F32),
            pltpu.VMEM((GROUP * rows, width), F32),
            *[pltpu.VMEM(m.shape, F32) for m in (mat_out, mat_fc1, mat_fc1)],
        ],
        total * 6 * width * (width + 2 * hidden_units),
    )


def run_back(tokens, counts, qkv, attend, d_mixed, d_middle, mat_qkv, vec):
    pairs, rows, deep, length, width, total = sizes_of(tokens)
    return run_pairs(
        functools.partial(back_kernel, length),
        tokens,
        counts,
        [
            ("image", tokens),
            ("pair", qkv),
            ("pair", attend),
            ("pair", d_mixed),
            ("pair", d_middle),
            ("whole", mat_qkv),
            ("whole", vec),
        ],
        [
            ("image", OF(tokens.shape, B16)),
            ("whole", OF(mat_qkv.shape, B16)),
            ("whole", OF(vec.shape, F32)),
        ],
        [
            pltpu.VMEM((GROUP * rows, width), F32),
            pltpu.VMEM((GROUP * rows, 3 * width), B16),
            pltpu.VMEM(mat_qkv.shape, F32),
        ],
        total * (12 * width * width + 8 * length * width),
    )


def groups():
    slow, fast = lax.axis_size("gx"), lax.axis_size("gy")
    cores = 2 if slow % 2 == 0 else 1
    return slow // cores, cores, fast


def part_of(part):
    sizes = groups()
    step = 1
    for size in sizes[part + 1 :]:
        step *= size
    return step, sizes[part], (lax.axis_index(AXES) // step) % sizes[part]


def swap(value, step):
    devices = lax.axis_size(AXES)
    return lax.ppermute(value, AXES, [(i, i ^ step) for i in range(devices)])


def send_whole(value, part):
    step, size, _ = part_of(part)
    return [value] + [swap(value, step * k) for k in range(1, size)]


def join(got, part, axis):
    _, size, at = part_of(part)
    shape = got[0].shape[:axis] + (size,) + got[0].shape[axis:]
    whole = jnp.zeros(shape, got[0].dtype)
    for k in range(size):
        whole = lax.dynamic_update_index_in_dim(whole, got[k], at ^ k, axis)
    return whole


def gather(value, part, axis):
    return join(send_whole(value, part), part, axis)


def cut(value, part, axis):
    _, size, at = part_of(part)
    value = value.astype(B16)
    return [lax.dynamic_index_in_dim(value, at ^ k, axis, keepdims=False) for k in range(size)]


def send_cut(blocks, part):
    step, _, _ = part_of(part)
    return blocks[:1] + [swap(block, step * k) for k, block in enumerate(blocks) if k]


def add_up(got):
    total = got[0].astype(F32)
    for block in got[1:]:
        total = total + block.astype(F32)
    return total


def scatter(value, part, axis):
    return add_up(send_cut(cut(value, part, axis), part))


def lanes_of(value):
    fill = -value.shape[-1] % (16 * LANES)
    if fill:
        value = jnp.pad(value, [(0, 0)] * (value.ndim - 1) + [(0, fill)])
    return value.reshape(value.shape[:-1] + (-1, LANES))


def body(tokens, counts, cotangent, w_qkv, w_out, w_fc1, w_fc2, gains, shifts, biases):
    width = tokens.shape[-1]
    devices = lax.axis_size(AXES)
    hidden_units = w_fc1.shape[0] * devices // width
    n_small = gains.shape[0] + shifts.shape[0] + biases.shape[0]
    cuts = [gains.shape[0], gains.shape[0] + shifts.shape[0]]

    small = jnp.concatenate([gains, shifts, biases])
    n_qkv = w_qkv.shape[0]
    first = gather(lanes_of(jnp.concatenate([w_qkv, small])), 0, 0)
    shards = [lanes_of(w) for w in (w_out, w_fc1, w_fc2)]
    n_rest = [w.shape[0] for w in shards]
    rest = gather(jnp.concatenate(shards), 0, 0)
    first = gather(gather(first, 2, 1), 1, 1)
    rest = gather(rest, 1, 1)
    first, rest = lax.optimization_barrier((first, rest))
    first = first.reshape((devices,) + first.shape[3:])
    rest = send_whole(rest, 2)

    def matrix(part, size, shape):
        return part.reshape(devices, -1)[:, :size].reshape(shape)

    mat_qkv = matrix(first, n_qkv, (width, 3 * width))
    small = first.reshape(devices, -1)[:, n_qkv : n_qkv + n_small].astype(F32)
    gain_all, shift_all, bias_all = [p.reshape(-1) for p in jnp.split(small, cuts, axis=1)]
    edge = 3 * width + hidden_units
    narrow = [
        gain_all.reshape(2, width),
        shift_all.reshape(2, width),
        bias_all[: 3 * width].reshape(3, width),
        bias_all[edge:].reshape(1, width),
    ]
    vec = jnp.concatenate(
        [
            jnp.pad(jnp.concatenate(narrow, axis=0), ((0, 0), (0, hidden_units - width))),
            bias_all[3 * width : edge].reshape(1, hidden_units),
            jnp.zeros((7, hidden_units), F32),
        ],
        axis=0,
    )

    counts = counts[0]
    qkv, attend, mixed = run_attend(tokens, counts, mat_qkv, vec)
    mixed, rest = lax.optimization_barrier((mixed, rest))
    rest = join(rest, 2, 2)
    rest = rest.reshape((devices,) + rest.shape[3:])
    cut_out, cut_fc1 = n_rest[0], n_rest[0] + n_rest[1]
    mat_out = matrix(rest[:, :cut_out], w_out.shape[0], (width, width))
    mat_fc1 = matrix(rest[:, cut_out:cut_fc1], w_fc1.shape[0], (width, hidden_units))
    mat_fc2 = matrix(rest[:, cut_fc1:], w_fc2.shape[0], (hidden_units, width))
    result, d_middle, d_mixed, g_out, g_fc1, g_fc2, g_vec_b = run_feed(
        tokens, counts, cotangent, mixed, mat_out, mat_fc1, mat_fc2, vec
    )
    flat = lambda whole: whole.reshape(devices, -1)
    parts = [lanes_of(flat(g)) for g in (g_out, g_fc1, g_fc2)]
    rest = jnp.concatenate(parts, axis=1)
    rest = cut(rest.reshape(groups() + rest.shape[1:]), 2, 2)
    d_mixed, rest = lax.optimization_barrier((d_mixed, rest))
    rest = send_cut(rest, 2)
    grad_tokens, g_qkv, g_vec_c = run_back(
        tokens, counts, qkv, attend, d_mixed, d_middle, mat_qkv, vec
    )
    g_qkv, rest = lax.optimization_barrier((g_qkv, rest))
    g_vec = g_vec_b + g_vec_c
    grad_biases = jnp.concatenate(
        [g_vec[4:7, :width].reshape(-1), g_vec[8], g_vec[7, :width]]
    )
    small = jnp.concatenate(
        [flat(g_vec[0:2, :width]), flat(g_vec[2:4, :width]), flat(grad_biases)], axis=1
    )
    first = lanes_of(jnp.concatenate([flat(g_qkv), small.astype(B16)], axis=1))
    first = scatter(first.reshape(groups() + first.shape[1:]), 1, 1)
    rest = scatter(add_up(rest), 1, 1)
    first = scatter(first, 2, 1)
    rest = scatter(rest, 0, 0)
    first = scatter(first, 0, 0)
    first = first.reshape(-1)
    grad_qkv = first[:n_qkv]
    grad_gains, grad_shifts, grad_biases = jnp.split(first[n_qkv : n_qkv + n_small], cuts)
    return (
        result,
        grad_tokens,
        grad_qkv,
        rest[:cut_out].reshape(-1)[: w_out.shape[0]],
        rest[cut_out:cut_fc1].reshape(-1)[: w_fc1.shape[0]],
        rest[cut_fc1:].reshape(-1)[: w_fc2.shape[0]],
        grad_gains,
        grad_shifts,
        grad_biases,
    )


def solution(mesh):
    return jax.shard_map(
        body,
        mesh=mesh,
        in_specs=(
            P(None, AXES, None, None),
            P(AXES, None),
            P(None, AXES, None, None),
            P(AXES),
            P(AXES),
            P(AXES),
            P(AXES),
            P(AXES),
            P(AXES),
            P(AXES),
        ),
        out_specs=(
            P(None, AXES, None, None),
            P(None, AXES, None, None),
            P(AXES),
            P(AXES),
            P(AXES),
            P(AXES),
            P(AXES),
            P(AXES),
            P(AXES),
        ),
        check_vma=False,
    )
```

```python
import functools

import jax
import jax.numpy as jnp
from jax import lax
from jax.experimental import pallas as pl
from jax.experimental.pallas import tpu as pltpu
from jax.sharding import PartitionSpec as P

HEAD = 64
EPS = 1e-06
F32 = jnp.float32
B16 = jnp.bfloat16
AXES = ("gx", "gy")
GROUP = 2
LANES = 128
OF = jax.ShapeDtypeStruct


def round_up(value, unit):
    return -(-value // unit) * unit


def dot(left, right):
    return jnp.dot(left, right, preferred_element_type=F32)


def dot_t(left, right):
    return lax.dot_general(left, right, (((1,), (1,)), ((), ())), preferred_element_type=F32)


def t_dot(left, right):
    return lax.dot_general(left, right, (((0,), (0,)), ((), ())), preferred_element_type=F32)


def norm_parts(values):
    center = values - jnp.mean(values, axis=-1, keepdims=True)
    factor = lax.rsqrt(jnp.mean(center * center, axis=-1, keepdims=True) + EPS)
    return center * factor, factor


def norm_back(incoming, unit, factor, gain):
    scaled = incoming * gain
    return factor * (
        scaled
        - jnp.mean(scaled, axis=-1, keepdims=True)
        - unit * jnp.mean(scaled * unit, axis=-1, keepdims=True)
    )


def colsum(values):
    return jnp.sum(values, axis=0, keepdims=True)


def gelu_both(hidden):
    size = jnp.abs(hidden)
    t = 1.0 / (1.0 + (0.3275911 * 0.5**0.5) * size)
    bell = jnp.exp(-0.5 * hidden * hidden)
    poly = t * (
        0.127414796
        + t * (-0.142248368 + t * (0.7107068705 + t * (-0.7265760135 + t * 0.5307027145)))
    )
    tail = poly * bell
    area = jnp.where(hidden >= 0, 1.0 - tail, tail)
    return hidden * area, area + hidden * (bell * 0.3989422804014327)


class Step:
    def __init__(self, plan):
        self.part, place = pl.program_id(0), pl.program_id(1)
        parts = pl.num_programs(0)
        self.own = self.part < parts - 1
        self.first = (self.part == 0) & (place == 0)
        self.last = (self.part == parts - 1) & (place == pl.num_programs(1) - 1)
        slot = (place + jnp.where(self.own, 0, plan[parts])) * GROUP
        self.alive = [slot + i < plan[self.part] for i in range(GROUP)]

    def load(self, into, own, other, length, masked=False):
        rows = into.shape[0] // GROUP
        for chosen, block in ((self.own, own), (jnp.logical_not(self.own), other)):

            @pl.when(chosen)
            def _():
                for i in range(GROUP):
                    values = block[0, i].astype(F32)
                    if masked:
                        values = values * self.alive[i].astype(F32)
                    into[i * rows : i * rows + length] = values

    def store(self, own, other, images):
        for i, image in enumerate(images):
            other[0, i] = image

        @pl.when(self.own)
        def _():
            for i, image in enumerate(images):
                own[0, i] = image

    def clear(self, own):
        @pl.when(jnp.logical_not(self.alive[0]) & self.own)
        def _():
            own[...] = jnp.zeros_like(own)


def halves(two, first_half):
    zero = jnp.zeros_like(two)
    return jnp.where(first_half, two, zero), jnp.where(first_half, zero, two)


def lower_lanes():
    return lax.broadcasted_iota(jnp.int32, (1, LANES), 1) < HEAD


def attend_kernel(length, plan, tok, tok_other, w_qkv, vec, qkv, attend, mixed, x_s):
    width = tok.shape[-1]
    rows = x_s.shape[0] // GROUP
    deep = qkv.shape[1] // GROUP
    pairs = width // LANES
    step = Step(plan)

    @pl.when(step.first)
    def _():
        x_s[...] = jnp.zeros_like(x_s)

    @pl.when(step.alive[0])
    def _():
        step.load(x_s, tok, tok_other, length)
        unit, _ = norm_parts(x_s[...])
        normed = (unit * vec[0:1, :width] + vec[2:3, :width]).astype(B16)
        queries = ((dot(normed, w_qkv[:, :width]) + vec[4:5, :width]) * HEAD**-0.5).astype(B16)
        keys_all = dot(normed, w_qkv[:, width : 2 * width]).astype(B16)
        values_all = (dot(normed, w_qkv[:, 2 * width :]) + vec[5:6, :width]).astype(B16)
        for i in range(GROUP):
            for at, part in enumerate((queries, keys_all, values_all)):
                cols = slice(at * width, (at + 1) * width)
                qkv[0, i * deep : i * deep + rows, cols] = part[i * rows : (i + 1) * rows]
            qkv[0, i * deep + rows : (i + 1) * deep] = jnp.zeros((deep - rows, 3 * width), B16)

        first_half = lower_lanes()
        tail = rows - 16
        hide = jnp.where(
            lax.broadcasted_iota(jnp.int32, (16, 1), 0) + tail < length, 0.0, -1e30
        ).astype(F32)
        blank = jnp.zeros((deep - rows, deep), B16)
        todo = [(i, pair) for i in range(GROUP) for pair in range(pairs)]

        def start(i, pair):
            q2 = qkv[0, pl.ds(i * deep, deep), pl.ds(pair * LANES, LANES)]
            k2 = qkv[0, pl.ds(i * deep, rows), pl.ds(width + pair * LANES, LANES)]
            return [dot_t(k2, q_one) for q_one in halves(q2, first_half)]

        def soften(i, pair, both):
            for half, scores in enumerate(both):
                scores = jnp.concatenate([scores[:tail], scores[tail:] + hide], axis=0)
                scores = jnp.exp(scores - jnp.max(scores, axis=0, keepdims=True))
                total = jnp.sum(scores, axis=0, keepdims=True)
                attend[0, i * 2 * pairs + 2 * pair + half] = (scores * (1.0 / total)).astype(B16)

        def mix(i, pair):
            v_t = qkv[0, pl.ds(i * deep, deep), pl.ds(2 * width + pair * LANES, LANES)].T
            parts = []
            for half in range(2):
                weights = attend[0, i * 2 * pairs + 2 * pair + half]
                mine = v_t[half * HEAD : (half + 1) * HEAD]
                parts.append(dot(mine, jnp.concatenate([weights, blank], axis=0)))
            mixed_two = jnp.concatenate(parts, axis=0).T
            mixed[0, pl.ds(i * rows, rows), pl.ds(pair * LANES, LANES)] = mixed_two[:rows].astype(B16)

        both = start(*todo[0])
        for at, here in enumerate(todo):
            after = start(*todo[at + 1]) if at + 1 < len(todo) else None
            soften(*here, both)
            if at:
                mix(*todo[at - 1])
            both = after
        mix(*todo[-1])


def feed_kernel(
    length, chunk, plan, tok, tok_other, cot, cot_other, mixed, w_out, w_fc1, w_fc2, vec,
    res, res_other, d_middle_out, d_mixed_out, o_out, o_fc1, o_fc2, g_vec, x_s, dy_s, g_out, g_fc1, g_fc2,
):
    width = tok.shape[-1]
    hidden_units = w_fc1.shape[1]
    rows = x_s.shape[0] // GROUP
    deep = d_mixed_out.shape[1] // GROUP
    step = Step(plan)

    @pl.when(step.first)
    def _():
        for ref in (x_s, dy_s, g_out, g_fc1, g_fc2, g_vec):
            ref[...] = jnp.zeros_like(ref)

    step.clear(res)

    @pl.when(step.alive[0])
    def _():
        step.load(x_s, tok, tok_other, length)
        step.load(dy_s, cot, cot_other, length, masked=True)
        gain, shift = vec[1:2, :width], vec[3:4, :width]
        middle = x_s[...] + dot(mixed[0], w_out[...]) + vec[6:7, :width]
        unit, factor = norm_parts(middle)
        normed = (unit * gain + shift).astype(B16)
        d_last = dy_s[...].astype(B16)
        last = vec[7:8, :width]
        d_normed = 0.0
        d_last_t, normed_t = d_last.T, normed.T
        starts = list(range(0, hidden_units, chunk))
        ahead, held = None, None
        for at in starts + [None] + [None]:
            if at is not None:
                cols = slice(at, at + chunk)
                hidden = dot(normed, w_fc1[:, cols]) + vec[8:9, cols]
                d_active = dot_t(d_last, w_fc2[cols, :])
            if held is not None:
                old, active_old, d_hidden_old = held
                last = last + dot(active_old, w_fc2[old, :])
                d_normed = d_normed + dot_t(d_hidden_old, w_fc1[:, old])
                g_fc2[:, old] += dot(d_last_t, active_old)
                g_fc1[:, old] += dot(normed_t, d_hidden_old)
                held = None
            if ahead is not None:
                now, hidden_now, d_active_now = ahead
                active, slope = gelu_both(hidden_now)
                active = active.astype(B16)
                d_hidden = d_active_now * slope
                g_vec[8:9, now] += colsum(d_hidden)
                d_hidden = d_hidden.astype(B16)
                held = (now, active, d_hidden)
            ahead = (cols, hidden, d_active) if at is not None else None
        result = middle + last
        images = [
            (result[i * rows : i * rows + length] * step.alive[i].astype(F32)).astype(B16)
            for i in range(GROUP)
        ]
        step.store(res, res_other, images)
        d_middle = dy_s[...] + norm_back(d_normed, unit, factor, gain)
        d_middle_out[0] = d_middle
        g_vec[1:2, :width] += colsum(d_normed * unit)
        g_vec[3:4, :width] += colsum(d_normed)
        g_vec[7:8, :width] += colsum(dy_s[...])
        g_vec[6:7, :width] += colsum(d_middle)
        d_branch = d_middle.astype(B16)
        g_out[...] += t_dot(mixed[0], d_branch)
        d_mixed = dot_t(d_branch, w_out[...]).astype(B16)
        for i in range(GROUP):
            d_mixed_out[0, i * deep : i * deep + rows] = d_mixed[i * rows : (i + 1) * rows]
            d_mixed_out[0, i * deep + rows : (i + 1) * deep] = jnp.zeros(
                (deep - rows, width), B16
            )

    @pl.when(step.last)
    def _():
        o_out[...] = g_out[...].astype(B16)
        o_fc1[...] = g_fc1[...].astype(B16)
        for at in range(0, hidden_units, width):
            o_fc2[at : at + width] = g_fc2[:, at : at + width].T.astype(B16)


def back_kernel(
    length, plan, tok, tok_other, qkv, attend, d_mixed, d_middle, w_qkv, vec, gtok, gtok_other, o_qkv, g_vec, x_s, dj_s, g_qkv
):
    width = tok.shape[-1]
    rows = x_s.shape[0] // GROUP
    deep = qkv.shape[1] // GROUP
    pairs = width // LANES
    step = Step(plan)

    @pl.when(step.first)
    def _():
        for ref in (x_s, g_qkv, g_vec):
            ref[...] = jnp.zeros_like(ref)

    step.clear(gtok)

    @pl.when(step.alive[0])
    def _():
        step.load(x_s, tok, tok_other, length)
        first_half = lower_lanes()
        blank = jnp.zeros((deep - rows, deep), B16)
        todo = [(i, pair) for i in range(GROUP) for pair in range(pairs)]

        def lanes_at(part, pair):
            return pl.ds(part * width + pair * LANES, LANES)

        def start(i, pair):
            v2 = qkv[0, pl.ds(i * deep, rows), lanes_at(2, pair)]
            m2 = d_mixed[0, pl.ds(i * deep, deep), lanes_at(0, pair)]
            return [dot_t(v2, m_one) for m_one in halves(m2, first_half)]

        def soften(i, pair, both):
            slopes = []
            for half, d_attend in enumerate(both):
                probs = attend[0, i * 2 * pairs + 2 * pair + half].astype(F32)
                product = probs * d_attend
                d_scores = product - probs * jnp.sum(product, axis=0, keepdims=True)
                slopes.append(d_scores.astype(B16))
            return slopes

        def finish(i, pair, slopes):
            q2 = qkv[0, pl.ds(i * deep, deep), lanes_at(0, pair)]
            k_t = qkv[0, pl.ds(i * deep, deep), lanes_at(1, pair)].T
            m2 = d_mixed[0, pl.ds(i * deep, deep), lanes_at(0, pair)]
            q_both, m_both = halves(q2, first_half), halves(m2, first_half)
            parts = [
                dot(
                    k_t[half * HEAD : (half + 1) * HEAD],
                    jnp.concatenate([slopes[half], blank], axis=0),
                )
                for half in range(2)
            ]
            attends = [attend[0, i * 2 * pairs + 2 * pair + half] for half in range(2)]
            d_queries = (jnp.concatenate(parts, axis=0) * HEAD**-0.5).T
            d_values = dot(jnp.concatenate(attends, axis=1), jnp.concatenate(m_both, axis=0))
            d_keys = dot(jnp.concatenate(slopes, axis=1), jnp.concatenate(q_both, axis=0))
            here = pl.ds(i * rows, rows)
            dj_s[here, lanes_at(0, pair)] = d_queries[:rows].astype(B16)
            dj_s[here, lanes_at(1, pair)] = d_keys.astype(B16)
            dj_s[here, lanes_at(2, pair)] = d_values.astype(B16)

        both, slopes = start(*todo[0]), None
        for at, here in enumerate(todo):
            after = start(*todo[at + 1]) if at + 1 < len(todo) else None
            if at:
                finish(*todo[at - 1], slopes)
            slopes = soften(*here, both)
            both = after
        finish(*todo[-1], slopes)

        gain = vec[0:1, :width]
        unit, factor = norm_parts(x_s[...])
        normed = (unit * gain + vec[2:3, :width]).astype(B16)
        g_vec[4:5, :width] += colsum(dj_s[:, :width].astype(F32))
        g_vec[5:6, :width] += colsum(dj_s[:, 2 * width :].astype(F32))
        g_qkv[...] += t_dot(normed, dj_s[...])
        d_normed = dot_t(dj_s[...], w_qkv[...])
        g_vec[0:1, :width] += colsum(d_normed * unit)
        g_vec[2:3, :width] += colsum(d_normed)
        d_input = d_middle[0] + norm_back(d_normed, unit, factor, gain)
        images = [d_input[i * rows : i * rows + length].astype(B16) for i in range(GROUP)]
        step.store(gtok, gtok_other, images)

    @pl.when(step.last)
    def _():
        o_qkv[...] = g_qkv[...].astype(B16)


def run_pairs(kernel, tokens, plan, inputs, outputs, scratch, flops):
    micro, slots, length, width = tokens.shape
    places = slots // GROUP

    def shift(m, c):
        return jnp.where(m == micro, c[micro + 1], 0)

    def near(m, p, c):
        last = (c[m] + GROUP - 1) // GROUP - shift(m, c) - 1
        return jnp.maximum(jnp.minimum(p, last), 0)

    def own_in(m, p, c):
        at = jnp.minimum(m, micro - 1)
        return (at, near(at, jnp.where(m == micro, places, p), c), 0, 0)

    def own_out(m, p, c):
        return (jnp.minimum(m, micro - 1), jnp.where(m == micro, places - 1, p), 0, 0)

    def other(m, p, c):
        return (0, c[micro + 1] + jnp.where(m == micro, near(micro, p, c), 0), 0, 0)

    def spec(kind, shape, out):
        block = (1, GROUP, length, width)
        if kind == "image":
            return pl.BlockSpec(block, own_out if out else own_in)
        if kind == "other":
            return pl.BlockSpec(block, other)
        if kind == "pair":
            rest = len(shape) - 1
            return pl.BlockSpec(
                (1, *shape[1:]), lambda m, p, c: (m * places + near(m, p, c),) + (0,) * rest
            )
        once = {} if out else {"pipeline_mode": pl.Buffered(1)}
        return pl.BlockSpec(shape, lambda m, p, c: (0,) * len(shape), **once)

    return pl.pallas_call(
        kernel,
        grid_spec=pltpu.PrefetchScalarGridSpec(
            num_scalar_prefetch=1,
            grid=(micro + 1, places),
            in_specs=[spec(kind, a.shape, False) for kind, a in inputs],
            out_specs=[spec(kind, a.shape, True) for kind, a in outputs],
            scratch_shapes=scratch,
        ),
        out_shape=[a for _, a in outputs],
        cost_estimate=pl.CostEstimate(
            flops=flops, bytes_accessed=64 * 2**20, transcendentals=0
        ),
        compiler_params=pltpu.CompilerParams(vmem_limit_bytes=56 * 2**20),
    )(plan, *[a for _, a in inputs])


def sizes_of(tokens):
    micro, slots, length, width = tokens.shape
    rows, deep = round_up(length, 16), round_up(length, LANES)
    pairs = (micro + 1) * slots // GROUP
    return pairs, rows, deep, length, width, micro * slots * length


def run_attend(tokens, tokens_other, plan, mat_qkv, vec):
    pairs, rows, deep, length, width, total = sizes_of(tokens)
    heads = width // HEAD
    return run_pairs(
        functools.partial(attend_kernel, length),
        tokens,
        plan,
        [("image", tokens), ("other", tokens_other), ("whole", mat_qkv), ("whole", vec)],
        [
            ("pair", OF((pairs, GROUP * deep, 3 * width), B16)),
            ("pair", OF((pairs, GROUP * heads, rows, deep), B16)),
            ("pair", OF((pairs, GROUP * rows, width), B16)),
        ],
        [pltpu.VMEM((GROUP * rows, width), F32)],
        total * (6 * width * width + 4 * length * width),
    )


def run_feed(tokens, tokens_other, plan, cotangent, cotangent_other, mixed, mat_out, mat_fc1, mat_fc2, vec):
    pairs, rows, deep, length, width, total = sizes_of(tokens)
    hidden_units = mat_fc1.shape[1]
    chunk = 256 if hidden_units % 256 == 0 else hidden_units
    matrices = (mat_out, mat_fc1, mat_fc2)
    return run_pairs(
        functools.partial(feed_kernel, length, chunk),
        tokens,
        plan,
        [
            ("image", tokens), ("other", tokens_other),
            ("image", cotangent), ("other", cotangent_other),
            ("pair", mixed),
            *[("whole", m) for m in matrices],
            ("whole", vec),
        ],
        [
            ("image", OF(tokens.shape, B16)), ("other", OF((1, *tokens.shape[1:]), B16)),
            ("pair", OF((pairs, GROUP * rows, width), F32)),
            ("pair", OF((pairs, GROUP * deep, width), B16)),
            *[("whole", OF(m.shape, B16)) for m in matrices],
            ("whole", OF(vec.shape, F32)),
        ],
        [
            pltpu.VMEM((GROUP * rows, width), F32),
            pltpu.VMEM((GROUP * rows, width), F32),
            *[pltpu.VMEM(m.shape, F32) for m in (mat_out, mat_fc1, mat_fc1)],
        ],
        total * 6 * width * (width + 2 * hidden_units),
    )


def run_back(tokens, tokens_other, plan, qkv, attend, d_mixed, d_middle, mat_qkv, vec):
    pairs, rows, deep, length, width, total = sizes_of(tokens)
    return run_pairs(
        functools.partial(back_kernel, length),
        tokens,
        plan,
        [
            ("image", tokens), ("other", tokens_other),
            ("pair", qkv),
            ("pair", attend),
            ("pair", d_mixed),
            ("pair", d_middle),
            ("whole", mat_qkv),
            ("whole", vec),
        ],
        [
            ("image", OF(tokens.shape, B16)), ("other", OF((1, *tokens.shape[1:]), B16)),
            ("whole", OF(mat_qkv.shape, B16)),
            ("whole", OF(vec.shape, F32)),
        ],
        [
            pltpu.VMEM((GROUP * rows, width), F32),
            pltpu.VMEM((GROUP * rows, 3 * width), B16),
            pltpu.VMEM(mat_qkv.shape, F32),
        ],
        total * (12 * width * width + 8 * length * width),
    )


def groups():
    slow, fast = lax.axis_size("gx"), lax.axis_size("gy")
    cores = 2 if slow % 2 == 0 else 1
    return slow // cores, cores, fast


def part_of(part):
    sizes = groups()
    step = 1
    for size in sizes[part + 1 :]:
        step *= size
    return step, sizes[part], (lax.axis_index(AXES) // step) % sizes[part]


def swap(value, step):
    devices = lax.axis_size(AXES)
    return lax.ppermute(value, AXES, [(i, i ^ step) for i in range(devices)])


def swap_core(value):
    step, size, _ = part_of(1)
    return swap(value, step) if size > 1 else value


def share(counts, slots):
    def filled(counts):
        pairs = (counts + GROUP - 1) // GROUP
        return pairs, jnp.argmax(pairs).astype(jnp.int32)

    def over(pairs, others, at):
        spare = (jnp.sum(pairs) - jnp.sum(others)) // 2
        return jnp.clip(spare, 0, pairs[at] - 1)

    others = swap_core(counts)
    pairs, at = filled(counts)
    their_pairs, their_at = filled(others)
    given = over(pairs, their_pairs, at)
    taken = over(their_pairs, pairs, their_at)
    keep = jnp.minimum(counts[at], (pairs[at] - given) * GROUP)
    mine = jnp.arange(counts.shape[0]) == at
    until = jnp.where(taken > 0, others[their_at], 0)
    since = jnp.where(taken > 0, their_pairs[their_at] - taken, 0)
    plan = jnp.concatenate([jnp.where(mine, keep, counts), until[None], since[None]])
    slot = jnp.arange(slots)[None, :]
    moved = mine[:, None] & (slot >= keep) & (slot < counts[at])
    return plan.astype(jnp.int32), at, moved


def send_whole(value, part):
    step, size, _ = part_of(part)
    return [value] + [swap(value, step * k) for k in range(1, size)]


def join(got, part, axis):
    _, size, at = part_of(part)
    shape = got[0].shape[:axis] + (size,) + got[0].shape[axis:]
    whole = jnp.zeros(shape, got[0].dtype)
    for k in range(size):
        whole = lax.dynamic_update_index_in_dim(whole, got[k], at ^ k, axis)
    return whole


def gather(value, part, axis):
    return join(send_whole(value, part), part, axis)


def cut(value, part, axis):
    _, size, at = part_of(part)
    value = value.astype(B16)
    return [lax.dynamic_index_in_dim(value, at ^ k, axis, keepdims=False) for k in range(size)]


def send_cut(blocks, part):
    step, _, _ = part_of(part)
    return blocks[:1] + [swap(block, step * k) for k, block in enumerate(blocks) if k]


def add_up(got):
    total = got[0].astype(F32)
    for block in got[1:]:
        total = total + block.astype(F32)
    return total


def scatter(value, part, axis):
    return add_up(send_cut(cut(value, part, axis), part))


def lanes_of(value):
    fill = -value.shape[-1] % (16 * LANES)
    if fill:
        value = jnp.pad(value, [(0, 0)] * (value.ndim - 1) + [(0, fill)])
    return value.reshape(value.shape[:-1] + (-1, LANES))


def body(tokens, counts, cotangent, w_qkv, w_out, w_fc1, w_fc2, gains, shifts, biases):
    width = tokens.shape[-1]
    devices = lax.axis_size(AXES)
    hidden_units = w_fc1.shape[0] * devices // width
    n_small = gains.shape[0] + shifts.shape[0] + biases.shape[0]
    cuts = [gains.shape[0], gains.shape[0] + shifts.shape[0]]

    plan, sent, moved = share(counts[0], tokens.shape[1])
    tokens_other, cotangent_other = [
        swap_core(lax.dynamic_slice_in_dim(a, sent, 1, axis=0)) for a in (tokens, cotangent)
    ]

    def merge(own, other):
        return jnp.where(moved[:, :, None, None], other, own)

    small = jnp.concatenate([gains, shifts, biases])
    n_qkv = w_qkv.shape[0]
    first = gather(lanes_of(jnp.concatenate([w_qkv, small])), 0, 0)
    shards = [lanes_of(w) for w in (w_out, w_fc1, w_fc2)]
    n_rest = [w.shape[0] for w in shards]
    rest = gather(jnp.concatenate(shards), 0, 0)
    first = gather(gather(first, 2, 1), 1, 1)
    rest = gather(rest, 1, 1)
    first, rest = lax.optimization_barrier((first, rest))
    first = first.reshape((devices,) + first.shape[3:])
    rest = send_whole(rest, 2)

    def matrix(part, size, shape):
        return part.reshape(devices, -1)[:, :size].reshape(shape)

    mat_qkv = matrix(first, n_qkv, (width, 3 * width))
    small = first.reshape(devices, -1)[:, n_qkv : n_qkv + n_small].astype(F32)
    gain_all, shift_all, bias_all = [p.reshape(-1) for p in jnp.split(small, cuts, axis=1)]
    edge = 3 * width + hidden_units
    narrow = [
        gain_all.reshape(2, width),
        shift_all.reshape(2, width),
        bias_all[: 3 * width].reshape(3, width),
        bias_all[edge:].reshape(1, width),
    ]
    vec = jnp.concatenate(
        [
            jnp.pad(jnp.concatenate(narrow, axis=0), ((0, 0), (0, hidden_units - width))),
            bias_all[3 * width : edge].reshape(1, hidden_units),
            jnp.zeros((7, hidden_units), F32),
        ],
        axis=0,
    )

    qkv, attend, mixed = run_attend(tokens, tokens_other, plan, mat_qkv, vec)
    mixed, rest, cotangent_other = lax.optimization_barrier((mixed, rest, cotangent_other))
    rest = join(rest, 2, 2)
    rest = rest.reshape((devices,) + rest.shape[3:])
    cut_out, cut_fc1 = n_rest[0], n_rest[0] + n_rest[1]
    mat_out = matrix(rest[:, :cut_out], w_out.shape[0], (width, width))
    mat_fc1 = matrix(rest[:, cut_out:cut_fc1], w_fc1.shape[0], (width, hidden_units))
    mat_fc2 = matrix(rest[:, cut_fc1:], w_fc2.shape[0], (hidden_units, width))
    result, result_other, d_middle, d_mixed, g_out, g_fc1, g_fc2, g_vec_b = run_feed(
        tokens, tokens_other, plan, cotangent, cotangent_other, mixed, mat_out, mat_fc1, mat_fc2, vec
    )
    flat = lambda whole: whole.reshape(devices, -1)
    parts = [lanes_of(flat(g)) for g in (g_out, g_fc1, g_fc2)]
    rest = jnp.concatenate(parts, axis=1)
    rest = cut(rest.reshape(groups() + rest.shape[1:]), 2, 2)
    d_mixed, rest, result_other = lax.optimization_barrier((d_mixed, rest, result_other))
    result_other = swap_core(result_other)
    rest = send_cut(rest, 2)
    grad_tokens, grad_other, g_qkv, g_vec_c = run_back(
        tokens, tokens_other, plan, qkv, attend, d_mixed, d_middle, mat_qkv, vec
    )
    g_qkv, rest, result_other = lax.optimization_barrier((g_qkv, rest, result_other))
    result = merge(result, result_other)
    grad_tokens = merge(grad_tokens, swap_core(grad_other))
    g_vec = g_vec_b + g_vec_c
    grad_biases = jnp.concatenate(
        [g_vec[4:7, :width].reshape(-1), g_vec[8], g_vec[7, :width]]
    )
    small = jnp.concatenate(
        [flat(g_vec[0:2, :width]), flat(g_vec[2:4, :width]), flat(grad_biases)], axis=1
    )
    first = lanes_of(jnp.concatenate([flat(g_qkv), small.astype(B16)], axis=1))
    first = scatter(first.reshape(groups() + first.shape[1:]), 1, 1)
    rest = scatter(add_up(rest), 1, 1)
    first = scatter(first, 2, 1)
    rest = scatter(rest, 0, 0)
    first = scatter(first, 0, 0)
    first = first.reshape(-1)
    grad_qkv = first[:n_qkv]
    grad_gains, grad_shifts, grad_biases = jnp.split(first[n_qkv : n_qkv + n_small], cuts)
    return (
        result,
        grad_tokens,
        grad_qkv,
        rest[:cut_out].reshape(-1)[: w_out.shape[0]],
        rest[cut_out:cut_fc1].reshape(-1)[: w_fc1.shape[0]],
        rest[cut_fc1:].reshape(-1)[: w_fc2.shape[0]],
        grad_gains,
        grad_shifts,
        grad_biases,
    )


def solution(mesh):
    return jax.shard_map(
        body,
        mesh=mesh,
        in_specs=(
            P(None, AXES, None, None),
            P(AXES, None),
            P(None, AXES, None, None),
            P(AXES),
            P(AXES),
            P(AXES),
            P(AXES),
            P(AXES),
            P(AXES),
            P(AXES),
        ),
        out_specs=(
            P(None, AXES, None, None),
            P(None, AXES, None, None),
            P(AXES),
            P(AXES),
            P(AXES),
            P(AXES),
            P(AXES),
            P(AXES),
            P(AXES),
        ),
        check_vma=False,
    )
```

```python
import functools

import jax
import jax.numpy as jnp
from jax import lax
from jax.experimental import pallas as pl
from jax.experimental.pallas import tpu as pltpu
from jax.sharding import PartitionSpec as P

HEAD = 64
EPS = 1e-06
F32 = jnp.float32
B16 = jnp.bfloat16
AXES = ("gx", "gy")
GROUP = 2
LANES = 128
OF = jax.ShapeDtypeStruct


def round_up(value, unit):
    return -(-value // unit) * unit


def dot(left, right):
    return jnp.dot(left, right, preferred_element_type=F32)


def dot_t(left, right):
    return lax.dot_general(left, right, (((1,), (1,)), ((), ())), preferred_element_type=F32)


def t_dot(left, right):
    return lax.dot_general(left, right, (((0,), (0,)), ((), ())), preferred_element_type=F32)


def norm_parts(values):
    center = values - jnp.mean(values, axis=-1, keepdims=True)
    factor = lax.rsqrt(jnp.mean(center * center, axis=-1, keepdims=True) + EPS)
    return center * factor, factor


def norm_back(incoming, unit, factor, gain):
    scaled = incoming * gain
    return factor * (
        scaled
        - jnp.mean(scaled, axis=-1, keepdims=True)
        - unit * jnp.mean(scaled * unit, axis=-1, keepdims=True)
    )


def colsum(values):
    return jnp.sum(values, axis=0, keepdims=True)


def gelu_both(hidden):
    size = jnp.abs(hidden)
    t = 1.0 / (1.0 + (0.3275911 * 0.5**0.5) * size)
    bell = jnp.exp(-0.5 * hidden * hidden)
    poly = t * (
        0.127414796
        + t * (-0.142248368 + t * (0.7107068705 + t * (-0.7265760135 + t * 0.5307027145)))
    )
    tail = poly * bell
    area = jnp.where(hidden >= 0, 1.0 - tail, tail)
    return hidden * area, area + hidden * (bell * 0.3989422804014327)


class Plan:
    def __init__(self, values, micro):
        self.ends = [values[m] for m in range(micro)]
        self.total, self.since = values[micro], values[micro + 1]
        self.limits = [values[micro + 2 + m] for m in range(micro + 1)]

    def own(self, step):
        step = jnp.minimum(step, self.ends[-1] - 1)
        part, base = 0, 0
        for end in self.ends[:-1]:
            part = part + (step >= end).astype(jnp.int32)
            base = jnp.where(step >= end, end, base)
        return part, step - base

    def other(self, step):
        step = jnp.minimum(step, self.total - 1)
        return self.since + jnp.maximum(step - self.ends[-1], 0)


class Step:
    def __init__(self, values, micro):
        plan = Plan(values, micro)
        step = pl.program_id(0)
        self.own = step < plan.ends[-1]
        self.first, self.last = step == 0, step == pl.num_programs(0) - 1
        self.active = step < plan.total
        part, place = plan.own(step)
        limit = plan.limits[0]
        for m in range(1, micro):
            limit = jnp.where(part == m, plan.limits[m], limit)
        slot = jnp.where(self.own, place, plan.other(step)) * GROUP
        limit = jnp.where(self.own, limit, plan.limits[micro])
        self.alive = [slot + i < limit for i in range(GROUP)]

    def load(self, into, own, other, length, masked=False):
        rows = into.shape[0] // GROUP
        for i in range(GROUP):
            values = jnp.where(self.own, own[0, i].astype(F32), other[0, i].astype(F32))
            if masked:
                values = values * self.alive[i].astype(F32)
            into[i * rows : i * rows + length] = values


def halves(two, first_half):
    zero = jnp.zeros_like(two)
    return jnp.where(first_half, two, zero), jnp.where(first_half, zero, two)


def lower_lanes():
    return lax.broadcasted_iota(jnp.int32, (1, LANES), 1) < HEAD


def attend_kernel(micro, length, plan, tok, tok_other, w_qkv, vec, qkv, attend, mixed, x_s):
    width = tok.shape[-1]
    rows = x_s.shape[0] // GROUP
    deep = qkv.shape[1] // GROUP
    pairs = width // LANES
    step = Step(plan, micro)

    @pl.when(step.first)
    def _():
        x_s[...] = jnp.zeros_like(x_s)

    @pl.when(step.active)
    def _():
        step.load(x_s, tok, tok_other, length)
        unit, _ = norm_parts(x_s[...])
        normed = (unit * vec[0:1, :width] + vec[2:3, :width]).astype(B16)
        queries = ((dot(normed, w_qkv[:, :width]) + vec[4:5, :width]) * HEAD**-0.5).astype(B16)
        keys_all = dot(normed, w_qkv[:, width : 2 * width]).astype(B16)
        values_all = (dot(normed, w_qkv[:, 2 * width :]) + vec[5:6, :width]).astype(B16)
        for i in range(GROUP):
            for at, part in enumerate((queries, keys_all, values_all)):
                cols = slice(at * width, (at + 1) * width)
                qkv[0, i * deep : i * deep + rows, cols] = part[i * rows : (i + 1) * rows]
            qkv[0, i * deep + rows : (i + 1) * deep] = jnp.zeros((deep - rows, 3 * width), B16)

        first_half = lower_lanes()
        tail = rows - 16
        hide = jnp.where(
            lax.broadcasted_iota(jnp.int32, (16, 1), 0) + tail < length, 0.0, -1e30
        ).astype(F32)
        blank = jnp.zeros((deep - rows, deep), B16)
        todo = [(i, pair) for i in range(GROUP) for pair in range(pairs)]

        def start(i, pair):
            q2 = qkv[0, pl.ds(i * deep, deep), pl.ds(pair * LANES, LANES)]
            k2 = qkv[0, pl.ds(i * deep, rows), pl.ds(width + pair * LANES, LANES)]
            return [dot_t(k2, q_one) for q_one in halves(q2, first_half)]

        def soften(i, pair, both):
            for half, scores in enumerate(both):
                scores = jnp.concatenate([scores[:tail], scores[tail:] + hide], axis=0)
                scores = jnp.exp(scores - jnp.max(scores, axis=0, keepdims=True))
                total = jnp.sum(scores, axis=0, keepdims=True)
                attend[0, i * 2 * pairs + 2 * pair + half] = (scores * (1.0 / total)).astype(B16)

        def mix(i, pair):
            v_t = qkv[0, pl.ds(i * deep, deep), pl.ds(2 * width + pair * LANES, LANES)].T
            parts = []
            for half in range(2):
                weights = attend[0, i * 2 * pairs + 2 * pair + half]
                mine = v_t[half * HEAD : (half + 1) * HEAD]
                parts.append(dot(mine, jnp.concatenate([weights, blank], axis=0)))
            mixed_two = jnp.concatenate(parts, axis=0).T
            mixed[0, pl.ds(i * rows, rows), pl.ds(pair * LANES, LANES)] = mixed_two[:rows].astype(B16)

        both = start(*todo[0])
        for at, here in enumerate(todo):
            after = start(*todo[at + 1]) if at + 1 < len(todo) else None
            soften(*here, both)
            if at:
                mix(*todo[at - 1])
            both = after
        mix(*todo[-1])


def feed_kernel(
    micro, length, chunk, plan, tok, tok_other, cot, cot_other, mixed, w_out, w_fc1, w_fc2, vec,
    res, d_middle_out, d_mixed_out, o_out, o_fc1, o_fc2, g_vec, x_s, dy_s, g_out, g_fc1, g_fc2,
):
    width = tok.shape[-1]
    hidden_units = w_fc1.shape[1]
    rows = x_s.shape[0] // GROUP
    deep = d_mixed_out.shape[1] // GROUP
    step = Step(plan, micro)

    @pl.when(step.first)
    def _():
        for ref in (x_s, dy_s, g_out, g_fc1, g_fc2, g_vec):
            ref[...] = jnp.zeros_like(ref)

    @pl.when(step.active)
    def _():
        step.load(x_s, tok, tok_other, length)
        step.load(dy_s, cot, cot_other, length, masked=True)
        gain, shift = vec[1:2, :width], vec[3:4, :width]
        middle = x_s[...] + dot(mixed[0], w_out[...]) + vec[6:7, :width]
        unit, factor = norm_parts(middle)
        normed = (unit * gain + shift).astype(B16)
        d_last = dy_s[...].astype(B16)
        last = vec[7:8, :width]
        d_normed = 0.0
        d_last_t, normed_t = d_last.T, normed.T
        starts = list(range(0, hidden_units, chunk))
        ahead, held = None, None
        for at in starts + [None] + [None]:
            if at is not None:
                cols = slice(at, at + chunk)
                hidden = dot(normed, w_fc1[:, cols]) + vec[8:9, cols]
                d_active = dot_t(d_last, w_fc2[cols, :])
            if held is not None:
                old, active_old, d_hidden_old = held
                last = last + dot(active_old, w_fc2[old, :])
                d_normed = d_normed + dot_t(d_hidden_old, w_fc1[:, old])
                g_fc2[:, old] += dot(d_last_t, active_old)
                g_fc1[:, old] += dot(normed_t, d_hidden_old)
                held = None
            if ahead is not None:
                now, hidden_now, d_active_now = ahead
                active, slope = gelu_both(hidden_now)
                active = active.astype(B16)
                d_hidden = d_active_now * slope
                g_vec[8:9, now] += colsum(d_hidden)
                d_hidden = d_hidden.astype(B16)
                held = (now, active, d_hidden)
            ahead = (cols, hidden, d_active) if at is not None else None
        result = middle + last
        for i in range(GROUP):
            image = result[i * rows : i * rows + length] * step.alive[i].astype(F32)
            res[0, i] = image.astype(B16)
        d_middle = dy_s[...] + norm_back(d_normed, unit, factor, gain)
        d_middle_out[0] = d_middle
        g_vec[1:2, :width] += colsum(d_normed * unit)
        g_vec[3:4, :width] += colsum(d_normed)
        g_vec[7:8, :width] += colsum(dy_s[...])
        g_vec[6:7, :width] += colsum(d_middle)
        d_branch = d_middle.astype(B16)
        g_out[...] += t_dot(mixed[0], d_branch)
        d_mixed = dot_t(d_branch, w_out[...]).astype(B16)
        for i in range(GROUP):
            d_mixed_out[0, i * deep : i * deep + rows] = d_mixed[i * rows : (i + 1) * rows]
            d_mixed_out[0, i * deep + rows : (i + 1) * deep] = jnp.zeros(
                (deep - rows, width), B16
            )

    @pl.when(step.last)
    def _():
        o_out[...] = g_out[...].astype(B16)
        o_fc1[...] = g_fc1[...].astype(B16)
        for at in range(0, hidden_units, width):
            o_fc2[at : at + width] = g_fc2[:, at : at + width].T.astype(B16)


def back_kernel(
    micro, length, plan, tok, tok_other, qkv, attend, d_mixed, d_middle, w_qkv, vec, gtok, o_qkv, g_vec, x_s, dj_s, g_qkv
):
    width = tok.shape[-1]
    rows = x_s.shape[0] // GROUP
    deep = qkv.shape[1] // GROUP
    pairs = width // LANES
    step = Step(plan, micro)

    @pl.when(step.first)
    def _():
        for ref in (x_s, g_qkv, g_vec):
            ref[...] = jnp.zeros_like(ref)

    @pl.when(step.active)
    def _():
        step.load(x_s, tok, tok_other, length)
        first_half = lower_lanes()
        blank = jnp.zeros((deep - rows, deep), B16)
        todo = [(i, pair) for i in range(GROUP) for pair in range(pairs)]

        def lanes_at(part, pair):
            return pl.ds(part * width + pair * LANES, LANES)

        def start(i, pair):
            v2 = qkv[0, pl.ds(i * deep, rows), lanes_at(2, pair)]
            m2 = d_mixed[0, pl.ds(i * deep, deep), lanes_at(0, pair)]
            return [dot_t(v2, m_one) for m_one in halves(m2, first_half)]

        def soften(i, pair, both):
            slopes = []
            for half, d_attend in enumerate(both):
                probs = attend[0, i * 2 * pairs + 2 * pair + half].astype(F32)
                product = probs * d_attend
                d_scores = product - probs * jnp.sum(product, axis=0, keepdims=True)
                slopes.append(d_scores.astype(B16))
            return slopes

        def finish(i, pair, slopes):
            q2 = qkv[0, pl.ds(i * deep, deep), lanes_at(0, pair)]
            k_t = qkv[0, pl.ds(i * deep, deep), lanes_at(1, pair)].T
            m2 = d_mixed[0, pl.ds(i * deep, deep), lanes_at(0, pair)]
            q_both, m_both = halves(q2, first_half), halves(m2, first_half)
            parts = [
                dot(
                    k_t[half * HEAD : (half + 1) * HEAD],
                    jnp.concatenate([slopes[half], blank], axis=0),
                )
                for half in range(2)
            ]
            attends = [attend[0, i * 2 * pairs + 2 * pair + half] for half in range(2)]
            d_queries = (jnp.concatenate(parts, axis=0) * HEAD**-0.5).T
            d_values = dot(jnp.concatenate(attends, axis=1), jnp.concatenate(m_both, axis=0))
            d_keys = dot(jnp.concatenate(slopes, axis=1), jnp.concatenate(q_both, axis=0))
            here = pl.ds(i * rows, rows)
            dj_s[here, lanes_at(0, pair)] = d_queries[:rows].astype(B16)
            dj_s[here, lanes_at(1, pair)] = d_keys.astype(B16)
            dj_s[here, lanes_at(2, pair)] = d_values.astype(B16)

        both, slopes = start(*todo[0]), None
        for at, here in enumerate(todo):
            after = start(*todo[at + 1]) if at + 1 < len(todo) else None
            if at:
                finish(*todo[at - 1], slopes)
            slopes = soften(*here, both)
            both = after
        finish(*todo[-1], slopes)

        gain = vec[0:1, :width]
        unit, factor = norm_parts(x_s[...])
        normed = (unit * gain + vec[2:3, :width]).astype(B16)
        g_vec[4:5, :width] += colsum(dj_s[:, :width].astype(F32))
        g_vec[5:6, :width] += colsum(dj_s[:, 2 * width :].astype(F32))
        g_qkv[...] += t_dot(normed, dj_s[...])
        d_normed = dot_t(dj_s[...], w_qkv[...])
        g_vec[0:1, :width] += colsum(d_normed * unit)
        g_vec[2:3, :width] += colsum(d_normed)
        d_input = d_middle[0] + norm_back(d_normed, unit, factor, gain)
        for i in range(GROUP):
            gtok[0, i] = d_input[i * rows : i * rows + length].astype(B16)

    @pl.when(step.last)
    def _():
        o_qkv[...] = g_qkv[...].astype(B16)


def run_pairs(kernel, tokens, plan, inputs, outputs, scratch, flops):
    micro, slots, length, width = tokens.shape

    def own(s, c):
        return (*Plan(c, micro).own(s), 0, 0)

    def other(s, c):
        return (0, Plan(c, micro).other(s), 0, 0)

    def both(s, c):
        plan = Plan(c, micro)
        part, place = plan.own(s)
        mine = jnp.minimum(s, plan.total - 1) < plan.ends[-1]
        return jnp.where(mine, part, micro), jnp.where(mine, place, plan.other(s)), 0, 0

    def spec(kind, shape, out):
        block = (1, GROUP, length, width)
        if kind == "image":
            return pl.BlockSpec(block, both if out else own)
        if kind == "other":
            return pl.BlockSpec(block, other)
        if kind == "pair":
            rest = (0,) * (len(shape) - 1)
            return pl.BlockSpec((1, *shape[1:]), lambda s, c: (jnp.minimum(s, c[micro] - 1), *rest))
        once = {} if out else {"pipeline_mode": pl.Buffered(1)}
        return pl.BlockSpec(shape, lambda s, c: (0,) * len(shape), **once)

    return pl.pallas_call(
        kernel,
        grid_spec=pltpu.PrefetchScalarGridSpec(
            num_scalar_prefetch=1,
            grid=(micro * slots // GROUP,),
            in_specs=[spec(kind, a.shape, False) for kind, a in inputs],
            out_specs=[spec(kind, a.shape, True) for kind, a in outputs],
            scratch_shapes=scratch,
        ),
        out_shape=[a for _, a in outputs],
        cost_estimate=pl.CostEstimate(
            flops=flops, bytes_accessed=64 * 2**20, transcendentals=0
        ),
        compiler_params=pltpu.CompilerParams(vmem_limit_bytes=56 * 2**20),
    )(plan, *[a for _, a in inputs])


def sizes_of(tokens):
    micro, slots, length, width = tokens.shape
    rows, deep = round_up(length, 16), round_up(length, LANES)
    pairs = micro * slots // GROUP
    return pairs, rows, deep, length, width, micro * slots * length


def run_attend(tokens, tokens_other, plan, mat_qkv, vec):
    pairs, rows, deep, length, width, total = sizes_of(tokens)
    heads = width // HEAD
    return run_pairs(
        functools.partial(attend_kernel, tokens.shape[0], length),
        tokens,
        plan,
        [("image", tokens), ("other", tokens_other), ("whole", mat_qkv), ("whole", vec)],
        [
            ("pair", OF((pairs, GROUP * deep, 3 * width), B16)),
            ("pair", OF((pairs, GROUP * heads, rows, deep), B16)),
            ("pair", OF((pairs, GROUP * rows, width), B16)),
        ],
        [pltpu.VMEM((GROUP * rows, width), F32)],
        total * (6 * width * width + 4 * length * width),
    )


def run_feed(tokens, tokens_other, plan, cotangent, cotangent_other, mixed, mat_out, mat_fc1, mat_fc2, vec):
    pairs, rows, deep, length, width, total = sizes_of(tokens)
    hidden_units = mat_fc1.shape[1]
    chunk = 256 if hidden_units % 256 == 0 else hidden_units
    matrices = (mat_out, mat_fc1, mat_fc2)
    return run_pairs(
        functools.partial(feed_kernel, tokens.shape[0], length, chunk),
        tokens,
        plan,
        [
            ("image", tokens), ("other", tokens_other),
            ("image", cotangent), ("other", cotangent_other),
            ("pair", mixed),
            *[("whole", m) for m in matrices],
            ("whole", vec),
        ],
        [
            ("image", OF((tokens.shape[0] + 1, *tokens.shape[1:]), B16)),
            ("pair", OF((pairs, GROUP * rows, width), F32)),
            ("pair", OF((pairs, GROUP * deep, width), B16)),
            *[("whole", OF(m.shape, B16)) for m in matrices],
            ("whole", OF(vec.shape, F32)),
        ],
        [
            pltpu.VMEM((GROUP * rows, width), F32),
            pltpu.VMEM((GROUP * rows, width), F32),
            *[pltpu.VMEM(m.shape, F32) for m in (mat_out, mat_fc1, mat_fc1)],
        ],
        total * 6 * width * (width + 2 * hidden_units),
    )


def run_back(tokens, tokens_other, plan, qkv, attend, d_mixed, d_middle, mat_qkv, vec):
    pairs, rows, deep, length, width, total = sizes_of(tokens)
    return run_pairs(
        functools.partial(back_kernel, tokens.shape[0], length),
        tokens,
        plan,
        [
            ("image", tokens), ("other", tokens_other),
            ("pair", qkv),
            ("pair", attend),
            ("pair", d_mixed),
            ("pair", d_middle),
            ("whole", mat_qkv),
            ("whole", vec),
        ],
        [
            ("image", OF((tokens.shape[0] + 1, *tokens.shape[1:]), B16)),
            ("whole", OF(mat_qkv.shape, B16)),
            ("whole", OF(vec.shape, F32)),
        ],
        [
            pltpu.VMEM((GROUP * rows, width), F32),
            pltpu.VMEM((GROUP * rows, 3 * width), B16),
            pltpu.VMEM(mat_qkv.shape, F32),
        ],
        total * (12 * width * width + 8 * length * width),
    )


def groups():
    slow, fast = lax.axis_size("gx"), lax.axis_size("gy")
    cores = 2 if slow % 2 == 0 else 1
    return slow // cores, cores, fast


def part_of(part):
    sizes = groups()
    step = 1
    for size in sizes[part + 1 :]:
        step *= size
    return step, sizes[part], (lax.axis_index(AXES) // step) % sizes[part]


def swap(value, step):
    devices = lax.axis_size(AXES)
    return lax.ppermute(value, AXES, [(i, i ^ step) for i in range(devices)])


def swap_core(value):
    step, size, _ = part_of(1)
    return swap(value, step) if size > 1 else value


def share(counts, slots):
    def filled(counts):
        pairs = (counts + GROUP - 1) // GROUP
        return pairs, jnp.argmax(pairs).astype(jnp.int32)

    def over(pairs, others, at):
        spare = (jnp.sum(pairs) - jnp.sum(others)) // 2
        return jnp.clip(spare, 0, pairs[at] - 1)

    micro = counts.shape[0]
    half = slots // 2 // GROUP

    def window(most):
        high = most > half
        return jnp.where(high, half, 0), jnp.where(high, most - half, most - 1)

    def surplus(total, other, most):
        return jnp.minimum(lax.div(jnp.maximum(total - other, 0), jnp.int32(2)), most)

    def fullest(counts):
        live = [counts[m] for m in range(micro)]
        pairs = [lax.div(c + (GROUP - 1), jnp.int32(GROUP)) for c in live]
        at, most, most_live = jnp.int32(0), pairs[0], live[0]
        for m in range(1, micro):
            better = pairs[m] > most
            at = jnp.where(better, jnp.int32(m), at)
            most = jnp.where(better, pairs[m], most)
            most_live = jnp.where(better, live[m], most_live)
        return live, pairs, sum(pairs[1:], pairs[0]), at, most, most_live

    live, pairs, total, at, most, most_live = fullest(counts)
    _, _, their_total, _, their_most, their_live = fullest(swap_core(counts))
    base, most = window(most)
    their_base, their_spare = window(their_most)
    given = surplus(total, their_total, most)
    taken = surplus(their_total, total, their_spare)
    ends, limits, end = [], [], jnp.int32(0)
    for m in range(micro):
        left = pairs[m] - jnp.where(at == m, given, 0)
        end = end + left
        ends.append(end)
        limits.append(jnp.minimum(live[m], left * GROUP))
    since = jnp.where(taken > 0, their_most - taken - their_base, 0)
    plan = jnp.stack(ends + [end + taken, since] + limits + [their_live - their_base * GROUP])
    slot = lax.broadcasted_iota(jnp.int32, (micro, slots), 1)
    part = lax.broadcasted_iota(jnp.int32, (micro, slots), 0)
    keep, alive = jnp.zeros((micro, slots), jnp.int32), jnp.zeros((micro, slots), jnp.int32)
    for m in range(micro):
        keep = jnp.where(part == m, limits[m], keep)
        alive = jnp.where(part == m, live[m], alive)
    return plan, (at, base > 0), (slot < keep, slot < alive)


def pick(array, at, high):
    half = array.shape[1] // 2
    one = lax.dynamic_index_in_dim(array, at, 0)
    return jnp.where(high, one[:, half:], one[:, :half])


def send_whole(value, part):
    step, size, _ = part_of(part)
    return [value] + [swap(value, step * k) for k in range(1, size)]


def join(got, part, axis):
    _, size, at = part_of(part)
    shape = got[0].shape[:axis] + (size,) + got[0].shape[axis:]
    whole = jnp.zeros(shape, got[0].dtype)
    for k in range(size):
        whole = lax.dynamic_update_index_in_dim(whole, got[k], at ^ k, axis)
    return whole


def gather(value, part, axis):
    return join(send_whole(value, part), part, axis)


def cut(value, part, axis):
    _, size, at = part_of(part)
    value = value.astype(B16)
    return [lax.dynamic_index_in_dim(value, at ^ k, axis, keepdims=False) for k in range(size)]


def send_cut(blocks, part):
    step, _, _ = part_of(part)
    return blocks[:1] + [swap(block, step * k) for k, block in enumerate(blocks) if k]


def add_up(got):
    total = got[0].astype(F32)
    for block in got[1:]:
        total = total + block.astype(F32)
    return total


def scatter(value, part, axis):
    return add_up(send_cut(cut(value, part, axis), part))


def lanes_of(value):
    fill = -value.shape[-1] % (16 * LANES)
    if fill:
        value = jnp.pad(value, [(0, 0)] * (value.ndim - 1) + [(0, fill)])
    return value.reshape(value.shape[:-1] + (-1, LANES))


def body(tokens, counts, cotangent, w_qkv, w_out, w_fc1, w_fc2, gains, shifts, biases):
    slots, width = tokens.shape[1], tokens.shape[-1]
    devices = lax.axis_size(AXES)
    hidden_units = w_fc1.shape[0] * devices // width
    n_small = gains.shape[0] + shifts.shape[0] + biases.shape[0]
    cuts = [gains.shape[0], gains.shape[0] + shifts.shape[0]]

    plan, sent, masks = share(counts[0], tokens.shape[1])
    tokens_other, cotangent_other = pick(tokens, *sent), pick(cotangent, *sent)

    def merge(own, other, masks):
        kept, live = [mask[:, :, None, None] for mask in masks]
        zero = jnp.zeros((), own.dtype)
        other = jnp.concatenate([other, other], axis=1)
        return jnp.where(kept, own[:-1], jnp.where(live, other, zero))

    small = jnp.concatenate([gains, shifts, biases])
    n_qkv = w_qkv.shape[0]
    shards = [lanes_of(w) for w in (w_out, w_fc1, w_fc2)]
    n_rest = [w.shape[0] for w in shards]
    rest = jnp.concatenate(shards)
    rest = lax.all_gather(rest, AXES)
    first = send_whole(lanes_of(jnp.concatenate([w_qkv, small])), 0)
    first, tokens_other = lax.optimization_barrier((first, tokens_other))
    first = send_whole(join(first, 0, 0), 2)
    tokens_other = swap_core(tokens_other)
    first, tokens_other = lax.optimization_barrier((first, tokens_other))
    first = join(send_whole(join(first, 2, 1), 1), 1, 1)
    cotangent_other = swap_core(cotangent_other)
    first = first.reshape((devices,) + first.shape[3:])

    def matrix(part, size, shape):
        return part.reshape(devices, -1)[:, :size].reshape(shape)

    mat_qkv = matrix(first, n_qkv, (width, 3 * width))
    small = first.reshape(devices, -1)[:, n_qkv : n_qkv + n_small].astype(F32)
    gain_all, shift_all, bias_all = [p.reshape(-1) for p in jnp.split(small, cuts, axis=1)]
    edge = 3 * width + hidden_units
    narrow = [
        gain_all.reshape(2, width),
        shift_all.reshape(2, width),
        bias_all[: 3 * width].reshape(3, width),
        bias_all[edge:].reshape(1, width),
    ]
    vec = jnp.concatenate(
        [
            jnp.pad(jnp.concatenate(narrow, axis=0), ((0, 0), (0, hidden_units - width))),
            bias_all[3 * width : edge].reshape(1, hidden_units),
            jnp.zeros((7, hidden_units), F32),
        ],
        axis=0,
    )

    qkv, attend, mixed = run_attend(tokens, tokens_other, plan, mat_qkv, vec)
    qkv, attend, mixed, rest, cotangent_other = lax.optimization_barrier(
        (qkv, attend, mixed, rest, cotangent_other)
    )
    cut_out, cut_fc1 = n_rest[0], n_rest[0] + n_rest[1]
    mat_out = matrix(rest[:, :cut_out], w_out.shape[0], (width, width))
    mat_fc1 = matrix(rest[:, cut_out:cut_fc1], w_fc1.shape[0], (width, hidden_units))
    mat_fc2 = matrix(rest[:, cut_fc1:], w_fc2.shape[0], (hidden_units, width))
    result, d_middle, d_mixed, g_out, g_fc1, g_fc2, g_vec_b = run_feed(
        tokens, tokens_other, plan, cotangent, cotangent_other, mixed, mat_out, mat_fc1, mat_fc2, vec
    )
    flat = lambda whole: whole.reshape(devices, -1)
    parts = [lanes_of(flat(g)) for g in (g_out, g_fc1, g_fc2)]
    rest = jnp.concatenate(parts, axis=1)
    rest = cut(rest.reshape(groups() + rest.shape[1:]), 2, 2)
    d_mixed, rest, result = lax.optimization_barrier((d_mixed, rest, result))
    result_other = swap_core(result[-1:, : slots // 2])
    rest = send_cut(rest, 2)
    grad_tokens, g_qkv, g_vec_c = run_back(
        tokens, tokens_other, plan, qkv, attend, d_mixed, d_middle, mat_qkv, vec
    )
    grad_tokens, g_qkv, g_vec_c, rest, result, result_other, g_vec_b, masks = (
        lax.optimization_barrier(
            (grad_tokens, g_qkv, g_vec_c, rest, result, result_other, g_vec_b, masks)
        )
    )
    grad_other = swap_core(grad_tokens[-1:, : slots // 2])
    g_vec = g_vec_b + g_vec_c
    grad_biases = jnp.concatenate(
        [g_vec[4:7, :width].reshape(-1), g_vec[8], g_vec[7, :width]]
    )
    small = jnp.concatenate(
        [flat(g_vec[0:2, :width]), flat(g_vec[2:4, :width]), flat(grad_biases)], axis=1
    )
    first = lanes_of(jnp.concatenate([flat(g_qkv), small.astype(B16)], axis=1))
    first = cut(first.reshape(groups() + first.shape[1:]), 1, 1)
    rest = cut(add_up(rest), 1, 1)
    n_first = first[0].shape[1] * first[0].shape[2]
    pairs = [
        jnp.concatenate([f.reshape(f.shape[0], n_first, LANES), r], axis=1)
        for f, r in zip(first, rest)
    ]
    both = add_up(send_cut(pairs, 1))
    result = merge(result, result_other, masks)
    result, both = lax.optimization_barrier((result, both))
    first = both[:, :n_first].reshape(both.shape[0], -1, first[0].shape[2], LANES)
    rest = both[:, n_first:]
    first = scatter(first, 2, 1)
    n_first = first.shape[1]
    both = scatter(jnp.concatenate([first, rest], axis=1), 0, 0)
    first, rest = both[:n_first], both[n_first:]
    grad_tokens = merge(grad_tokens, grad_other, masks)
    first = first.reshape(-1)
    grad_qkv = first[:n_qkv]
    grad_gains, grad_shifts, grad_biases = jnp.split(first[n_qkv : n_qkv + n_small], cuts)
    return (
        result,
        grad_tokens,
        grad_qkv,
        rest[:cut_out].reshape(-1)[: w_out.shape[0]],
        rest[cut_out:cut_fc1].reshape(-1)[: w_fc1.shape[0]],
        rest[cut_fc1:].reshape(-1)[: w_fc2.shape[0]],
        grad_gains,
        grad_shifts,
        grad_biases,
    )


def solution(mesh):
    return jax.shard_map(
        body,
        mesh=mesh,
        in_specs=(
            P(None, AXES, None, None),
            P(AXES, None),
            P(None, AXES, None, None),
            P(AXES),
            P(AXES),
            P(AXES),
            P(AXES),
            P(AXES),
            P(AXES),
            P(AXES),
        ),
        out_specs=(
            P(None, AXES, None, None),
            P(None, AXES, None, None),
            P(AXES),
            P(AXES),
            P(AXES),
            P(AXES),
            P(AXES),
            P(AXES),
            P(AXES),
        ),
        check_vma=False,
    )
```

```python
import functools

import jax
import jax.numpy as jnp
from jax import lax
from jax.experimental import pallas as pl
from jax.experimental.pallas import tpu as pltpu
from jax.sharding import PartitionSpec as P

HEAD = 64
EPS = 1e-06
F32 = jnp.float32
B16 = jnp.bfloat16
AXES = ("gx", "gy")
GROUP = 2
LANES = 128
OF = jax.ShapeDtypeStruct


def round_up(value, unit):
    return -(-value // unit) * unit


def dot(left, right):
    return jnp.dot(left, right, preferred_element_type=F32)


def dot_t(left, right):
    return lax.dot_general(left, right, (((1,), (1,)), ((), ())), preferred_element_type=F32)


def t_dot(left, right):
    return lax.dot_general(left, right, (((0,), (0,)), ((), ())), preferred_element_type=F32)


def norm_parts(values):
    center = values - jnp.mean(values, axis=-1, keepdims=True)
    factor = lax.rsqrt(jnp.mean(center * center, axis=-1, keepdims=True) + EPS)
    return center * factor, factor


def norm_back(incoming, unit, factor, gain):
    scaled = incoming * gain
    return factor * (
        scaled
        - jnp.mean(scaled, axis=-1, keepdims=True)
        - unit * jnp.mean(scaled * unit, axis=-1, keepdims=True)
    )


def colsum(values):
    return jnp.sum(values, axis=0, keepdims=True)


def gelu_both(hidden):
    size = jnp.abs(hidden)
    t = 1.0 / (1.0 + (0.3275911 * 0.5**0.5) * size)
    bell = jnp.exp(-0.5 * hidden * hidden)
    poly = t * (
        0.127414796
        + t * (-0.142248368 + t * (0.7107068705 + t * (-0.7265760135 + t * 0.5307027145)))
    )
    tail = poly * bell
    area = jnp.where(hidden >= 0, 1.0 - tail, tail)
    return hidden * area, area + hidden * (bell * 0.3989422804014327)


def put_rows(x_s, block, rows, length):
    for i in range(GROUP):
        x_s[i * rows : i * rows + length] = block[0, i].astype(F32)


def halves(two, first_half):
    zero = jnp.zeros_like(two)
    return jnp.where(first_half, two, zero), jnp.where(first_half, zero, two)


def lower_lanes():
    return lax.broadcasted_iota(jnp.int32, (1, LANES), 1) < HEAD


def attend_kernel(length, counts, tok, w_qkv, vec, qkv, attend, mixed, x_s):
    width = tok.shape[-1]
    rows = x_s.shape[0] // GROUP
    deep = qkv.shape[1] // GROUP
    pairs = width // LANES
    micro, place = pl.program_id(0), pl.program_id(1)

    @pl.when((micro == 0) & (place == 0))
    def _():
        x_s[...] = jnp.zeros_like(x_s)

    @pl.when(place * GROUP < counts[micro])
    def _():
        put_rows(x_s, tok, rows, length)
        unit, _ = norm_parts(x_s[...])
        normed = (unit * vec[0:1, :width] + vec[2:3, :width]).astype(B16)
        queries = ((dot(normed, w_qkv[:, :width]) + vec[4:5, :width]) * HEAD**-0.5).astype(B16)
        keys_all = dot(normed, w_qkv[:, width : 2 * width]).astype(B16)

        def keep(at, part):
            for i in range(GROUP):
                cols = slice(at * width, (at + 1) * width)
                qkv[0, i * deep : i * deep + rows, cols] = part[i * rows : (i + 1) * rows]
                qkv[0, i * deep + rows : (i + 1) * deep, cols] = jnp.zeros(
                    (deep - rows, width), B16
                )

        keep(0, queries)
        keep(1, keys_all)
        first_half = lower_lanes()
        tail = rows - 16
        hide = jnp.where(
            lax.broadcasted_iota(jnp.int32, (16, 1), 0) + tail < length, 0.0, -1e30
        ).astype(F32)
        blank = jnp.zeros((deep - rows, deep), B16)
        todo = [(i, pair) for i in range(GROUP) for pair in range(pairs)]

        def start(i, pair):
            q2 = qkv[0, pl.ds(i * deep, deep), pl.ds(pair * LANES, LANES)]
            k2 = qkv[0, pl.ds(i * deep, rows), pl.ds(width + pair * LANES, LANES)]
            return [dot_t(k2, q_one) for q_one in halves(q2, first_half)]

        def soften(i, pair, both):
            for half, scores in enumerate(both):
                scores = jnp.concatenate([scores[:tail], scores[tail:] + hide], axis=0)
                scores = jnp.exp(scores - jnp.max(scores, axis=0, keepdims=True))
                total = jnp.sum(scores, axis=0, keepdims=True)
                attend[0, i * 2 * pairs + 2 * pair + half] = (scores * (1.0 / total)).astype(B16)

        def mix(i, pair):
            v_t = qkv[0, pl.ds(i * deep, deep), pl.ds(2 * width + pair * LANES, LANES)].T
            parts = []
            for half in range(2):
                weights = attend[0, i * 2 * pairs + 2 * pair + half]
                mine = v_t[half * HEAD : (half + 1) * HEAD]
                parts.append(dot(mine, jnp.concatenate([weights, blank], axis=0)))
            mixed_two = jnp.concatenate(parts, axis=0).T
            mixed[0, pl.ds(i * rows, rows), pl.ds(pair * LANES, LANES)] = mixed_two[:rows].astype(B16)

        both = start(*todo[0])
        values_all = (dot(normed, w_qkv[:, 2 * width :]) + vec[5:6, :width]).astype(B16)
        keep(2, values_all)
        for at, here in enumerate(todo):
            after = start(*todo[at + 1]) if at + 1 < len(todo) else None
            soften(*here, both)
            if at:
                mix(*todo[at - 1])
            both = after
        mix(*todo[-1])


def feed_kernel(
    length, chunk, counts, tok, cot, mixed, w_out, w_fc1, w_fc2, vec,
    res, d_middle_out, d_mixed_out, o_out, o_fc1, o_fc2, g_vec, x_s, dy_s, g_out, g_fc1, g_fc2,
):
    width = tok.shape[-1]
    hidden_units = w_fc1.shape[1]
    rows = x_s.shape[0] // GROUP
    deep = d_mixed_out.shape[1] // GROUP
    micro, place = pl.program_id(0), pl.program_id(1)
    live_count = counts[micro]

    @pl.when((micro == 0) & (place == 0))
    def _():
        for ref in (x_s, dy_s, g_out, g_fc1, g_fc2, g_vec):
            ref[...] = jnp.zeros_like(ref)

    @pl.when(place * GROUP >= live_count)
    def _():
        res[...] = jnp.zeros_like(res)

    @pl.when(place * GROUP < live_count)
    def _():
        put_rows(x_s, tok, rows, length)
        for i in range(GROUP):
            live = (place * GROUP + i < live_count).astype(F32)
            dy_s[i * rows : i * rows + length] = cot[0, i].astype(F32) * live
        gain, shift = vec[1:2, :width], vec[3:4, :width]
        middle = x_s[...] + dot(mixed[0], w_out[...]) + vec[6:7, :width]
        unit, factor = norm_parts(middle)
        normed = (unit * gain + shift).astype(B16)
        d_last = dy_s[...].astype(B16)
        last = vec[7:8, :width]
        d_normed = 0.0
        d_last_t, normed_t = d_last.T, normed.T
        starts = list(range(0, hidden_units, chunk))
        ahead, held = None, None
        for at in starts + [None] + [None]:
            if at is not None:
                cols = slice(at, at + chunk)
                hidden = dot(normed, w_fc1[:, cols]) + vec[8:9, cols]
                d_active = dot_t(d_last, w_fc2[cols, :])
            if held is not None:
                old, active_old, d_hidden_old = held
                last = last + dot(active_old, w_fc2[old, :])
                d_normed = d_normed + dot_t(d_hidden_old, w_fc1[:, old])
                g_fc2[:, old] += dot(d_last_t, active_old)
                g_fc1[:, old] += dot(normed_t, d_hidden_old)
                held = None
            if ahead is not None:
                now, hidden_now, d_active_now = ahead
                active, slope = gelu_both(hidden_now)
                active = active.astype(B16)
                d_hidden = d_active_now * slope
                g_vec[8:9, now] += colsum(d_hidden)
                d_hidden = d_hidden.astype(B16)
                held = (now, active, d_hidden)
            ahead = (cols, hidden, d_active) if at is not None else None
        result = middle + last
        for i in range(GROUP):
            live = (place * GROUP + i < live_count).astype(F32)
            res[0, i] = (result[i * rows : i * rows + length] * live).astype(B16)
        d_middle = dy_s[...] + norm_back(d_normed, unit, factor, gain)
        d_middle_out[0] = d_middle
        g_vec[1:2, :width] += colsum(d_normed * unit)
        g_vec[3:4, :width] += colsum(d_normed)
        g_vec[7:8, :width] += colsum(dy_s[...])
        g_vec[6:7, :width] += colsum(d_middle)
        d_branch = d_middle.astype(B16)
        g_out[...] += t_dot(mixed[0], d_branch)
        d_mixed = dot_t(d_branch, w_out[...]).astype(B16)
        for i in range(GROUP):
            d_mixed_out[0, i * deep : i * deep + rows] = d_mixed[i * rows : (i + 1) * rows]
            d_mixed_out[0, i * deep + rows : (i + 1) * deep] = jnp.zeros(
                (deep - rows, width), B16
            )

    @pl.when(last_step())
    def _():
        o_out[...] = g_out[...].astype(B16)
        o_fc1[...] = g_fc1[...].astype(B16)
        for at in range(0, hidden_units, width):
            o_fc2[at : at + width] = g_fc2[:, at : at + width].T.astype(B16)


def last_step():
    return (pl.program_id(0) == pl.num_programs(0) - 1) & (
        pl.program_id(1) == pl.num_programs(1) - 1
    )


def back_kernel(
    length, counts, tok, qkv, attend, d_mixed, d_middle, w_qkv, vec, gtok, o_qkv, g_vec, x_s, dj_s, g_qkv
):
    width = tok.shape[-1]
    rows = x_s.shape[0] // GROUP
    deep = qkv.shape[1] // GROUP
    pairs = width // LANES
    micro, place = pl.program_id(0), pl.program_id(1)

    @pl.when((micro == 0) & (place == 0))
    def _():
        for ref in (x_s, g_qkv, g_vec):
            ref[...] = jnp.zeros_like(ref)

    @pl.when(place * GROUP >= counts[micro])
    def _():
        gtok[...] = jnp.zeros_like(gtok)

    @pl.when(place * GROUP < counts[micro])
    def _():
        put_rows(x_s, tok, rows, length)
        first_half = lower_lanes()
        blank = jnp.zeros((deep - rows, deep), B16)
        todo = [(i, pair) for i in range(GROUP) for pair in range(pairs)]

        def lanes_at(part, pair):
            return pl.ds(part * width + pair * LANES, LANES)

        def start(i, pair):
            v2 = qkv[0, pl.ds(i * deep, rows), lanes_at(2, pair)]
            m2 = d_mixed[0, pl.ds(i * deep, deep), lanes_at(0, pair)]
            return [dot_t(v2, m_one) for m_one in halves(m2, first_half)]

        def soften(i, pair, both):
            slopes = []
            for half, d_attend in enumerate(both):
                probs = attend[0, i * 2 * pairs + 2 * pair + half].astype(F32)
                product = probs * d_attend
                d_scores = product - probs * jnp.sum(product, axis=0, keepdims=True)
                slopes.append(d_scores.astype(B16))
            return slopes

        def finish(i, pair, slopes):
            q2 = qkv[0, pl.ds(i * deep, deep), lanes_at(0, pair)]
            k_t = qkv[0, pl.ds(i * deep, deep), lanes_at(1, pair)].T
            m2 = d_mixed[0, pl.ds(i * deep, deep), lanes_at(0, pair)]
            q_both, m_both = halves(q2, first_half), halves(m2, first_half)
            parts = [
                dot(
                    k_t[half * HEAD : (half + 1) * HEAD],
                    jnp.concatenate([slopes[half], blank], axis=0),
                )
                for half in range(2)
            ]
            attends = [attend[0, i * 2 * pairs + 2 * pair + half] for half in range(2)]
            d_queries = (jnp.concatenate(parts, axis=0) * HEAD**-0.5).T
            d_values = dot(jnp.concatenate(attends, axis=1), jnp.concatenate(m_both, axis=0))
            d_keys = dot(jnp.concatenate(slopes, axis=1), jnp.concatenate(q_both, axis=0))
            here = pl.ds(i * rows, rows)
            dj_s[here, lanes_at(0, pair)] = d_queries[:rows].astype(B16)
            dj_s[here, lanes_at(1, pair)] = d_keys.astype(B16)
            dj_s[here, lanes_at(2, pair)] = d_values.astype(B16)

        both, slopes = start(*todo[0]), None
        for at, here in enumerate(todo):
            after = start(*todo[at + 1]) if at + 1 < len(todo) else None
            if at:
                finish(*todo[at - 1], slopes)
            slopes = soften(*here, both)
            both = after
        finish(*todo[-1], slopes)

        gain = vec[0:1, :width]
        unit, factor = norm_parts(x_s[...])
        normed = (unit * gain + vec[2:3, :width]).astype(B16)
        g_vec[4:5, :width] += colsum(dj_s[:, :width].astype(F32))
        g_vec[5:6, :width] += colsum(dj_s[:, 2 * width :].astype(F32))
        d_normed = dot_t(dj_s[...], w_qkv[...])
        g_qkv[...] += t_dot(normed, dj_s[...])
        g_vec[0:1, :width] += colsum(d_normed * unit)
        g_vec[2:3, :width] += colsum(d_normed)
        d_input = d_middle[0] + norm_back(d_normed, unit, factor, gain)
        for i in range(GROUP):
            gtok[0, i] = d_input[i * rows : i * rows + length].astype(B16)

    @pl.when(last_step())
    def _():
        o_qkv[...] = g_qkv[...].astype(B16)


def run_pairs(kernel, tokens, counts, inputs, outputs, scratch, flops):
    micro, slots, length, width = tokens.shape
    places = slots // GROUP

    def near(m, p, c):
        return jnp.minimum(p, (c[m] - 1) // GROUP)

    def spec(kind, shape, out):
        if kind == "image":
            block = (1, GROUP, length, width)
            if out:
                return pl.BlockSpec(block, lambda m, p, c: (m, p, 0, 0))
            return pl.BlockSpec(block, lambda m, p, c: (m, near(m, p, c), 0, 0))
        if kind == "pair":
            rest = len(shape) - 1
            return pl.BlockSpec(
                (1, *shape[1:]), lambda m, p, c: (m * places + near(m, p, c),) + (0,) * rest
            )
        once = {} if out else {"pipeline_mode": pl.Buffered(1)}
        return pl.BlockSpec(shape, lambda m, p, c: (0,) * len(shape), **once)

    return pl.pallas_call(
        kernel,
        grid_spec=pltpu.PrefetchScalarGridSpec(
            num_scalar_prefetch=1,
            grid=(micro, places),
            in_specs=[spec(kind, a.shape, False) for kind, a in inputs],
            out_specs=[spec(kind, a.shape, True) for kind, a in outputs],
            scratch_shapes=scratch,
        ),
        out_shape=[a for _, a in outputs],
        cost_estimate=pl.CostEstimate(
            flops=flops, bytes_accessed=64 * 2**20, transcendentals=0
        ),
        compiler_params=pltpu.CompilerParams(vmem_limit_bytes=56 * 2**20),
    )(counts, *[a for _, a in inputs])


def sizes_of(tokens):
    micro, slots, length, width = tokens.shape
    rows, deep = round_up(length, 16), round_up(length, LANES)
    return micro * slots // GROUP, rows, deep, length, width, micro * slots * length


def run_attend(tokens, counts, mat_qkv, vec):
    pairs, rows, deep, length, width, total = sizes_of(tokens)
    heads = width // HEAD
    return run_pairs(
        functools.partial(attend_kernel, length),
        tokens,
        counts,
        [("image", tokens), ("whole", mat_qkv), ("whole", vec)],
        [
            ("pair", OF((pairs, GROUP * deep, 3 * width), B16)),
            ("pair", OF((pairs, GROUP * heads, rows, deep), B16)),
            ("pair", OF((pairs, GROUP * rows, width), B16)),
        ],
        [pltpu.VMEM((GROUP * rows, width), F32)],
        total * (6 * width * width + 4 * length * width),
    )


def run_feed(tokens, counts, cotangent, mixed, mat_out, mat_fc1, mat_fc2, vec):
    pairs, rows, deep, length, width, total = sizes_of(tokens)
    hidden_units = mat_fc1.shape[1]
    chunk = 256 if hidden_units % 256 == 0 else hidden_units
    matrices = (mat_out, mat_fc1, mat_fc2)
    return run_pairs(
        functools.partial(feed_kernel, length, chunk),
        tokens,
        counts,
        [
            ("image", tokens),
            ("image", cotangent),
            ("pair", mixed),
            *[("whole", m) for m in matrices],
            ("whole", vec),
        ],
        [
            ("image", OF(tokens.shape, B16)),
            ("pair", OF((pairs, GROUP * rows, width), F32)),
            ("pair", OF((pairs, GROUP * deep, width), B16)),
            *[("whole", OF(m.shape, B16)) for m in matrices],
            ("whole", OF(vec.shape, F32)),
        ],
        [
            pltpu.VMEM((GROUP * rows, width), F32),
            pltpu.VMEM((GROUP * rows, width), F32),
            *[pltpu.VMEM(m.shape, F32) for m in (mat_out, mat_fc1, mat_fc1)],
        ],
        total * 6 * width * (width + 2 * hidden_units),
    )


def run_back(tokens, counts, qkv, attend, d_mixed, d_middle, mat_qkv, vec):
    pairs, rows, deep, length, width, total = sizes_of(tokens)
    return run_pairs(
        functools.partial(back_kernel, length),
        tokens,
        counts,
        [
            ("image", tokens),
            ("pair", qkv),
            ("pair", attend),
            ("pair", d_mixed),
            ("pair", d_middle),
            ("whole", mat_qkv),
            ("whole", vec),
        ],
        [
            ("image", OF(tokens.shape, B16)),
            ("whole", OF(mat_qkv.shape, B16)),
            ("whole", OF(vec.shape, F32)),
        ],
        [
            pltpu.VMEM((GROUP * rows, width), F32),
            pltpu.VMEM((GROUP * rows, 3 * width), B16),
            pltpu.VMEM(mat_qkv.shape, F32),
        ],
        total * (12 * width * width + 8 * length * width),
    )


def groups():
    slow, fast = lax.axis_size("gx"), lax.axis_size("gy")
    cores = 2 if slow % 2 == 0 else 1
    return slow // cores, cores, fast


def part_of(part):
    sizes = groups()
    step = 1
    for size in sizes[part + 1 :]:
        step *= size
    return step, sizes[part], (lax.axis_index(AXES) // step) % sizes[part]


def swap(value, step):
    devices = lax.axis_size(AXES)
    return lax.ppermute(value, AXES, [(i, i ^ step) for i in range(devices)])


def send_whole(value, part):
    step, size, _ = part_of(part)
    return [value] + [swap(value, step * k) for k in range(1, size)]


def join(got, part, axis):
    _, size, at = part_of(part)
    shape = got[0].shape[:axis] + (size,) + got[0].shape[axis:]
    whole = jnp.zeros(shape, got[0].dtype)
    for k in range(size):
        whole = lax.dynamic_update_index_in_dim(whole, got[k], at ^ k, axis)
    return whole


def gather(value, part, axis):
    return join(send_whole(value, part), part, axis)


def cut(value, part, axis):
    _, size, at = part_of(part)
    value = value.astype(B16)
    return [lax.dynamic_index_in_dim(value, at ^ k, axis, keepdims=False) for k in range(size)]


def send_cut(blocks, part):
    step, _, _ = part_of(part)
    return blocks[:1] + [swap(block, step * k) for k, block in enumerate(blocks) if k]


def add_up(got):
    total = got[0].astype(F32)
    for block in got[1:]:
        total = total + block.astype(F32)
    return total


def scatter(value, part, axis):
    return add_up(send_cut(cut(value, part, axis), part))


def lanes_of(value):
    fill = -value.shape[-1] % (16 * LANES)
    if fill:
        value = jnp.pad(value, [(0, 0)] * (value.ndim - 1) + [(0, fill)])
    return value.reshape(value.shape[:-1] + (-1, LANES))


def body(tokens, counts, cotangent, w_qkv, w_out, w_fc1, w_fc2, gains, shifts, biases):
    width = tokens.shape[-1]
    devices = lax.axis_size(AXES)
    hidden_units = w_fc1.shape[0] * devices // width
    n_small = gains.shape[0] + shifts.shape[0] + biases.shape[0]
    cuts = [gains.shape[0], gains.shape[0] + shifts.shape[0]]

    small = jnp.concatenate([gains, shifts, biases])
    n_qkv = w_qkv.shape[0]
    first = gather(lanes_of(jnp.concatenate([w_qkv, small])), 0, 0)
    shards = [lanes_of(w) for w in (w_out, w_fc1, w_fc2)]
    n_rest = [w.shape[0] for w in shards]
    rest = gather(jnp.concatenate(shards), 0, 0)
    first = gather(gather(first, 2, 1), 1, 1)
    rest = gather(rest, 1, 1)
    first, rest = lax.optimization_barrier((first, rest))
    first = first.reshape((devices,) + first.shape[3:])
    rest = send_whole(rest, 2)

    def matrix(part, size, shape):
        return part.reshape(devices, -1)[:, :size].reshape(shape)

    mat_qkv = matrix(first, n_qkv, (width, 3 * width))
    small = first.reshape(devices, -1)[:, n_qkv : n_qkv + n_small].astype(F32)
    gain_all, shift_all, bias_all = [p.reshape(-1) for p in jnp.split(small, cuts, axis=1)]
    edge = 3 * width + hidden_units
    narrow = [
        gain_all.reshape(2, width),
        shift_all.reshape(2, width),
        bias_all[: 3 * width].reshape(3, width),
        bias_all[edge:].reshape(1, width),
    ]
    vec = jnp.concatenate(
        [
            jnp.pad(jnp.concatenate(narrow, axis=0), ((0, 0), (0, hidden_units - width))),
            bias_all[3 * width : edge].reshape(1, hidden_units),
            jnp.zeros((7, hidden_units), F32),
        ],
        axis=0,
    )

    counts = counts[0]
    qkv, attend, mixed = run_attend(tokens, counts, mat_qkv, vec)
    mixed, rest = lax.optimization_barrier((mixed, rest))
    rest = join(rest, 2, 2)
    rest = rest.reshape((devices,) + rest.shape[3:])
    cut_out, cut_fc1 = n_rest[0], n_rest[0] + n_rest[1]
    mat_out = matrix(rest[:, :cut_out], w_out.shape[0], (width, width))
    mat_fc1 = matrix(rest[:, cut_out:cut_fc1], w_fc1.shape[0], (width, hidden_units))
    mat_fc2 = matrix(rest[:, cut_fc1:], w_fc2.shape[0], (hidden_units, width))
    result, d_middle, d_mixed, g_out, g_fc1, g_fc2, g_vec_b = run_feed(
        tokens, counts, cotangent, mixed, mat_out, mat_fc1, mat_fc2, vec
    )
    flat = lambda whole: whole.reshape(devices, -1)
    parts = [lanes_of(flat(g)) for g in (g_out, g_fc1, g_fc2)]
    rest = jnp.concatenate(parts, axis=1)
    rest = cut(rest.reshape(groups() + rest.shape[1:]), 2, 2)
    d_mixed, rest = lax.optimization_barrier((d_mixed, rest))
    rest = send_cut(rest, 2)
    grad_tokens, g_qkv, g_vec_c = run_back(
        tokens, counts, qkv, attend, d_mixed, d_middle, mat_qkv, vec
    )
    g_qkv, rest = lax.optimization_barrier((g_qkv, rest))
    g_vec = g_vec_b + g_vec_c
    grad_biases = jnp.concatenate(
        [g_vec[4:7, :width].reshape(-1), g_vec[8], g_vec[7, :width]]
    )
    small = jnp.concatenate(
        [flat(g_vec[0:2, :width]), flat(g_vec[2:4, :width]), flat(grad_biases)], axis=1
    )
    first = lanes_of(jnp.concatenate([flat(g_qkv), small.astype(B16)], axis=1))
    first = cut(first.reshape(groups() + first.shape[1:]), 1, 1)
    rest = cut(add_up(rest), 1, 1)
    n_first = first[0].shape[1] * first[0].shape[2]
    joined = [
        jnp.concatenate([f.reshape(f.shape[0], n_first, LANES), r], axis=1)
        for f, r in zip(first, rest)
    ]
    both = add_up(send_cut(joined, 1))
    first = both[:, :n_first].reshape(both.shape[0], -1, first[0].shape[2], LANES)
    rest = both[:, n_first:]
    first = scatter(first, 2, 1)
    n_first = first.shape[1]
    both = scatter(jnp.concatenate([first, rest], axis=1), 0, 0)
    first, rest = both[:n_first], both[n_first:]
    first = first.reshape(-1)
    grad_qkv = first[:n_qkv]
    grad_gains, grad_shifts, grad_biases = jnp.split(first[n_qkv : n_qkv + n_small], cuts)
    return (
        result,
        grad_tokens,
        grad_qkv,
        rest[:cut_out].reshape(-1)[: w_out.shape[0]],
        rest[cut_out:cut_fc1].reshape(-1)[: w_fc1.shape[0]],
        rest[cut_fc1:].reshape(-1)[: w_fc2.shape[0]],
        grad_gains,
        grad_shifts,
        grad_biases,
    )


def solution(mesh):
    return jax.shard_map(
        body,
        mesh=mesh,
        in_specs=(
            P(None, AXES, None, None),
            P(AXES, None),
            P(None, AXES, None, None),
            P(AXES),
            P(AXES),
            P(AXES),
            P(AXES),
            P(AXES),
            P(AXES),
            P(AXES),
        ),
        out_specs=(
            P(None, AXES, None, None),
            P(None, AXES, None, None),
            P(AXES),
            P(AXES),
            P(AXES),
            P(AXES),
            P(AXES),
            P(AXES),
            P(AXES),
        ),
        check_vma=False,
    )
```
